512 devices in a mesh: crop: 16 (over y, x_lo, core), res: 32 (over z, x_hi).
Axes of the slice: x: 4 (x_hi: 2, x_lo: 2; x = x_hi * 2 + x_lo), y: 4, z: 16, core: 2. Of those that a mesh axis runs over, the one named last changes fastest.
Arguments:
- alignment: bfloat16 [2048, 64, 256], P('crop', 'res'), parts along dimension 0, may hold values from -6 to 6
- pair_features: bfloat16 [64, 1024, 128], P('res', 'crop'), parts along dimension 1, may hold values from -6 to 6
- pair_cotangent: bfloat16 [64, 1024, 128], P('res', 'crop'), parts along dimension 1, may hold values from -6 to 6
- outer_weight: bfloat16 [256, 64], replicated, may hold values from -1 to 1
- mean_weight: bfloat16 [1024, 128], replicated, may hold values from -0.1875 to 0.1875
- triangle_weight: bfloat16 [2, 128, 512], replicated, may hold values from -0.5 to 0.5
- gating_weight: bfloat16 [2, 128, 128], replicated, may hold values from -0.5 to 0.5
- mixing_weight: bfloat16 [2, 128, 128], replicated, may hold values from -0.5 to 0.5
Outputs:
- updated_pair: bfloat16 [64, 1024, 128], P('res', 'crop'), parts along dimension 1
- alignment_gradient: float32 [2048, 64, 256], P('crop', 'res'), parts along dimension 0
- pair_gradient: float32 [64, 1024, 128], P('res', 'crop'), parts along dimension 1
- outer_gradient: float32 [4096, 64], P('crop'), parts along dimension 0
- mean_gradient: float32 [16384, 128], P('crop'), parts along dimension 0
- triangle_gradient: float32 [32, 128, 512], P('crop'), parts along dimension 0
- gating_gradient: float32 [32, 128, 128], P('crop'), parts along dimension 0
- mixing_gradient: float32 [32, 128, 128], P('crop'), parts along dimension 0
The draws below stay inside these ranges and needn't reach their ends.
There are 16 independent parts, one for each index of `crop`. The reference program is written for one: setup_inputs(seed, part) draws one part's arguments, and reference() takes and returns one part's arrays. A program takes and returns all parts, laid end to end along the dimension named above; an argument that names none is the same for every part. Nothing has to cross between parts.
All inputs are finite; a program needn't handle non-finite values.
Results may differ from the reference program's by a relative error of at most 0.035.
Values may be sent and summed in bfloat16 or wider, within the bound.
A program may use at most 64 MiB of HBM per device.

```python
import jax
import jax.numpy as jnp
from jax import lax

C_M = 256
C_Z = 128
C_OUTER = 32
C_TRI = 128
SEQS = 128
RESIDUES = 64


def levels(rng, extent, pieces, smallest, top_value):
    level = 1.0
    for position, blocks in pieces:
        heights = jax.random.uniform(jax.random.fold_in(jax.random.fold_in(rng, 6), position), (blocks,), jnp.float32, smallest / len(pieces), top_value / len(pieces))
        level = level * jnp.repeat(jnp.exp(heights), extent[position] // blocks).reshape((-1,) + (1,) * (len(extent) - 1 - position))
    return level


def noise(rng, extent, spread, most, cuts=(), kind=jnp.bfloat16):
    result = jax.random.normal(rng, extent, jnp.float32) * spread
    if len(cuts) > 0:
        result = levels(rng, extent, cuts, -0.22, 0.18) * result
    return jnp.clip(result, min=-most, max=most).astype(kind)


def setup_inputs(seed: int = 0, part: int = 0) -> dict:
    key_of = jax.random.split(jax.random.key(seed), 9)
    own_keys = jax.random.split(jax.random.fold_in(key_of[8], part), 9)
    return {
        "alignment": noise(own_keys[0], (SEQS, RESIDUES, C_M), 1.0, 6.0, ((1, 32),)),
        "pair_features": noise(own_keys[1], (RESIDUES, RESIDUES, C_Z), 1.0, 6.0, ((0, 32),)),
        "pair_cotangent": noise(own_keys[2], (RESIDUES, RESIDUES, C_Z), 1.0, 6.0, ((0, 32),)),
        "outer_weight": noise(key_of[3], (C_M, 2 * C_OUTER), (C_M // 8) ** -0.5, 1.0),
        "mean_weight": noise(key_of[4], (C_OUTER * C_OUTER, C_Z), (C_OUTER * C_OUTER) ** -0.5, 0.1875),
        "triangle_weight": noise(key_of[5], (2, C_Z, 4 * C_TRI), C_Z ** -0.5, 0.5),
        "gating_weight": noise(key_of[6], (2, C_Z, C_Z), C_Z ** -0.5, 0.5),
        "mixing_weight": noise(key_of[7], (2, C_TRI, C_Z), C_TRI ** -0.5, 0.5),
    }


EPS = 1e-05
HIGHEST = lax.Precision.HIGHEST

def normalize(values):
    center = lax.optimization_barrier(jnp.mean(values, axis=-1, keepdims=True))
    shifted = values - center
    inverse = lax.rsqrt(lax.optimization_barrier(jnp.mean(shifted * shifted, axis=-1, keepdims=True)) + EPS)
    return (shifted * inverse, inverse)

def norm_back(normed, inverse, upstream):
    mean_upstream = lax.optimization_barrier(jnp.mean(upstream, axis=-1, keepdims=True))
    mean_product = lax.optimization_barrier(jnp.mean(upstream * normed, axis=-1, keepdims=True))
    return inverse * (upstream - mean_upstream - normed * mean_product)

def project(values, weight):
    columns = values.shape[-1]
    flattened = jnp.dot(values.reshape(-1, columns), weight, preferred_element_type=jnp.float32)
    return flattened.reshape(values.shape[:-1] + (weight.shape[1],))

def back_project(upstream, weight):
    columns = upstream.shape[-1]
    flattened = jnp.dot(upstream.reshape(-1, columns), weight.T, preferred_element_type=jnp.float32)
    return flattened.reshape(upstream.shape[:-1] + (weight.shape[0],))

def weight_gradient(values, upstream):
    flat_values = values.reshape(-1, values.shape[-1])
    flat_upstream = upstream.reshape(-1, upstream.shape[-1])
    return jnp.dot(flat_values.T, flat_upstream, preferred_element_type=jnp.float32)

def triangle_head(pair_block, project_weight, gate_weight):
    normed, inverse = normalize(pair_block.astype(jnp.float32))
    normed_half = normed.astype(jnp.bfloat16)
    projected = project(normed_half, project_weight)
    quarter = project_weight.shape[1] // 4
    linear_left = projected[..., :quarter]
    switch_left = jax.nn.sigmoid(projected[..., quarter:2 * quarter])
    linear_right = projected[..., 2 * quarter:3 * quarter]
    switch_right = jax.nn.sigmoid(projected[..., 3 * quarter:])
    left_factor = (switch_left * linear_left).astype(jnp.bfloat16)
    right_factor = (switch_right * linear_right).astype(jnp.bfloat16)
    gating = jax.nn.sigmoid(project(normed_half, gate_weight))
    saved = (normed, inverse, normed_half, linear_left, switch_left, linear_right, switch_right)
    return (left_factor, right_factor, gating, saved)

def triangle_tail(pair_block, mixed, gating, mixing):
    mixed_norm, mixed_inverse = normalize(mixed)
    mixed_half = mixed_norm.astype(jnp.bfloat16)
    update = project(mixed_half, mixing)
    updated = (pair_block.astype(jnp.float32) + gating * update).astype(jnp.bfloat16)
    return (updated, (mixed_norm, mixed_inverse, mixed_half, update))

def tail_backward(upstream, gating, saved, mixing):
    mixed_norm, mixed_inverse, mixed_half, update = saved
    update_gradient = (upstream * gating).astype(jnp.bfloat16)
    logit_gradient = (upstream * update * gating * (1.0 - gating)).astype(jnp.bfloat16)
    mixing_grads = weight_gradient(mixed_half, update_gradient)
    mixed_gradient = norm_back(mixed_norm, mixed_inverse, back_project(update_gradient, mixing)).astype(jnp.bfloat16)
    return (mixed_gradient, logit_gradient, mixing_grads)

def head_backward(upstream, saved, left_gradient, right_gradient, logit_gradient, project_weight, gate_weight):
    normed, inverse, normed_half, linear_left, switch_left, linear_right, switch_right = saved
    left_wide = left_gradient.astype(jnp.float32)
    right_wide = right_gradient.astype(jnp.float32)
    quarter_gradient = jnp.concatenate([left_wide * switch_left, left_wide * linear_left * switch_left * (1.0 - switch_left), right_wide * switch_right, right_wide * linear_right * switch_right * (1.0 - switch_right)], axis=-1).astype(jnp.bfloat16)
    project_grads = weight_gradient(normed_half, quarter_gradient)
    gate_grads = weight_gradient(normed_half, logit_gradient)
    normed_gradient = back_project(quarter_gradient, project_weight) + back_project(logit_gradient, gate_weight)
    return (upstream + norm_back(normed, inverse, normed_gradient), project_grads, gate_grads)

def product(form, first, second):
    return jnp.einsum(form, first.astype(jnp.float32), second.astype(jnp.float32), precision=HIGHEST)

def reference(alignment, pair_features, pair_cotangent, outer_weight, mean_weight, triangle_weight, gating_weight, mixing_weight):
    sequences = alignment.shape[0]
    channels = outer_weight.shape[1] // 2
    residues = pair_features.shape[0]
    aligned_norm, aligned_inverse = normalize(alignment.astype(jnp.float32))
    aligned_half = aligned_norm.astype(jnp.bfloat16)
    projected = project(aligned_half, outer_weight).astype(jnp.bfloat16)
    outer_left = projected[..., :channels]
    outer_right = projected[..., channels:]
    outer_mean = (product('sia,sjb->ijab', outer_left, outer_right) / sequences).reshape(residues, residues, channels * channels).astype(jnp.bfloat16)
    first_pair = (pair_features.astype(jnp.float32) + project(outer_mean, mean_weight)).astype(jnp.bfloat16)
    first_left, first_right, first_gating, first_head = triangle_head(first_pair, triangle_weight[0], gating_weight[0])
    second_pair, first_tail = triangle_tail(first_pair, product('ikc,jkc->ijc', first_left, first_right), first_gating, mixing_weight[0])
    second_left, second_right, second_gating, second_head = triangle_head(second_pair, triangle_weight[1], gating_weight[1])
    updated_pair, second_tail = triangle_tail(second_pair, product('kic,kjc->ijc', second_left, second_right), second_gating, mixing_weight[1])
    upstream = pair_cotangent.astype(jnp.float32)
    mixed_gradient, logit_gradient, second_mixing = tail_backward(upstream, second_gating, second_tail, mixing_weight[1])
    left_gradient = product('ijc,kjc->kic', mixed_gradient, second_right).astype(jnp.bfloat16)
    right_gradient = product('ijc,kic->kjc', mixed_gradient, second_left).astype(jnp.bfloat16)
    second_gradient, second_project, second_gate = head_backward(upstream, second_head, left_gradient, right_gradient, logit_gradient, triangle_weight[1], gating_weight[1])
    mixed_gradient, logit_gradient, first_mixing = tail_backward(second_gradient, first_gating, first_tail, mixing_weight[0])
    left_gradient = product('ijc,jkc->ikc', mixed_gradient, first_right).astype(jnp.bfloat16)
    right_gradient = product('ijc,ikc->jkc', mixed_gradient, first_left).astype(jnp.bfloat16)
    first_gradient, first_project, first_gate = head_backward(second_gradient, first_head, left_gradient, right_gradient, logit_gradient, triangle_weight[0], gating_weight[0])
    mean_cotangent = first_gradient.astype(jnp.bfloat16)
    mean_gradient = weight_gradient(outer_mean, mean_cotangent)
    outer_cotangent = (back_project(mean_cotangent, mean_weight) / sequences).astype(jnp.bfloat16).reshape(residues, residues, channels, channels)
    outer_left_gradient = product('ijab,sjb->sia', outer_cotangent, outer_right)
    outer_right_gradient = product('ijab,sia->sjb', outer_cotangent, outer_left)
    projection_gradient = jnp.concatenate([outer_left_gradient, outer_right_gradient], axis=-1).astype(jnp.bfloat16)
    outer_gradient = weight_gradient(aligned_half, projection_gradient)
    alignment_gradient = norm_back(aligned_norm, aligned_inverse, back_project(projection_gradient, outer_weight))
    return (updated_pair, alignment_gradient, first_gradient, outer_gradient, mean_gradient, jnp.stack([first_project, second_project]), jnp.stack([first_gate, second_gate]), jnp.stack([first_mixing, second_mixing]))
```

```python
import functools

import jax
import jax.numpy as jnp
from jax import lax
from jax.experimental import pallas as pl
from jax.experimental.pallas import tpu as pltpu
from jax.sharding import PartitionSpec as P

EPS = 1e-05
F32 = jnp.float32
BF16 = jnp.bfloat16
MESH = pl.DeviceIdType.MESH

DEVICES = 32
ROWS = 2
RES = DEVICES * ROWS
CELLS = ROWS * RES
CH = 128
OUT = 32
SEQ = 128
MSA = 256
PER = CH // DEVICES
EARLY = 1024
LATE = 2048

NN = (((1,), (0,)), ((), ()))
NT = (((1,), (1,)), ((), ()))
TN = (((0,), (0,)), ((), ()))


def mul(a, b, dims=NN):
    return lax.dot_general(a, b, dims, preferred_element_type=F32)


def normalize(values, axis):
    shifted = values - jnp.mean(values, axis=axis, keepdims=True)
    inverse = lax.rsqrt(jnp.mean(shifted * shifted, axis=axis, keepdims=True) + EPS)
    return shifted * inverse, inverse


def norm_back(normed, inverse, upstream, axis):
    mean_upstream = jnp.mean(upstream, axis=axis, keepdims=True)
    mean_product = jnp.mean(upstream * normed, axis=axis, keepdims=True)
    return inverse * (upstream - mean_upstream - normed * mean_product)


def kernel(
    alignment_ref, pair_ref, cotangent_ref, outer_ref, mean_ref, mean_swapped_ref, triangle_ref, gating_ref, mixing_ref,
    updated_ref, alignment_grad_ref, pair_grad_ref, outer_grad_ref, mean_grad_ref, triangle_grad_ref, gating_grad_ref,
    mixing_grad_ref,
    left_own, right_own, left_all, right_all, aligned, aligned_inv, spread, outer_mean, pack,
    factor_send, factor_recv, mixed_send, mixed_recv, back_send, back_recv, grad_send, grad_recv, cot_send, cot_recv,
    left_chan, right_chan, triangle_t, normed_s, parts_s, gate_s, tail_s, logit_s, upstream_s,
    early_send, early_recv, early_own, early_all, late_send, late_recv, late_own, late_all,
    send_sem, recv_sem,
):
    me = lax.axis_index("res")
    other = lax.rem(me + 1, DEVICES)

    def each_peer(body):
        def step(k, carry):
            body(lax.rem(me + k, DEVICES))
            return carry

        lax.fori_loop(1, DEVICES, step, 0)

    def remote(source, target, phase, peer):
        return pltpu.make_async_remote_copy(
            src_ref=source, dst_ref=target, send_sem=send_sem.at[phase], recv_sem=recv_sem.at[phase],
            device_id={"res": peer}, device_id_type=MESH,
        )

    def exchange(send, recv, phase):
        each_peer(lambda peer: remote(send.at[peer], recv.at[me], phase, peer).start())
        recv[me] = send[me]

    def arrived(recv, phase):
        view = recv.at[pl.ds(0, DEVICES - 1)]
        remote(view, view, phase, other).wait_recv()

    def sent(send, phase):
        view = send.at[pl.ds(0, DEVICES - 1)]
        remote(view, view, phase, other).wait_send()

    barrier = pltpu.get_barrier_semaphore()
    each_peer(lambda peer: pl.semaphore_signal(barrier, inc=1, device_id={"res": peer}, device_id_type=MESH))

    for j in range(ROWS):
        normed, inverse = normalize(alignment_ref[j].astype(F32), 1)
        aligned[j] = normed
        aligned_inv[j] = inverse
        projected = mul(outer_ref[...], normed.astype(BF16), (((0,), (1,)), ((), ()))).astype(BF16)
        left_own[j] = projected[:OUT]
        right_own[j] = projected[OUT:]
    pl.semaphore_wait(barrier, DEVICES - 1)

    each_peer(lambda peer: remote(right_own, right_all.at[:, me], 0, peer).start())
    right_all[:, me] = right_own[...]
    each_peer(lambda peer: remote(left_own, left_all.at[:, me], 1, peer).start())
    left_all[:, me] = left_own[...]

    row = lax.broadcasted_iota(jnp.int32, (CELLS, CELLS), 0)
    column = lax.broadcasted_iota(jnp.int32, (CELLS, CELLS), 1)
    place = (row // RES) * RES + lax.rem(row, 2) * DEVICES + lax.rem(row, RES) // 2
    order = jnp.where(place == column, 1.0, 0.0).astype(BF16)
    pair = mul(pair_ref[...], order, TN)
    upstream_s[0] = mul(cotangent_ref[...], order, TN)
    for t in range(2):
        triangle_t[t, : 4 * CH] = triangle_ref[t].T
        triangle_t[t, 4 * CH : 5 * CH] = gating_ref[t].T
        triangle_t[t, 5 * CH :] = mixing_ref[t].T
    pack[...] = jnp.zeros_like(pack)
    early_send[...] = jnp.zeros_like(early_send)
    late_send[...] = jnp.zeros_like(late_send)

    def put(values, slot):
        for k in range(PER):
            pack[pl.ds(slot + k, DEVICES, stride=8), :] = values[k * DEVICES : (k + 1) * DEVICES]

    def post(send):
        send[...] = pack[...].reshape(DEVICES, 8, CELLS).astype(BF16)

    def take(recv):
        pack[...] = recv[...].astype(F32).reshape(DEVICES * 8, CELLS)

    def get(slot):
        return jnp.concatenate([pack[pl.ds(slot + k, DEVICES, stride=8), :] for k in range(PER)], axis=0)

    def channel(slot):
        values = pack[pl.ds(slot, DEVICES, stride=8), :]
        return jnp.concatenate([values[:, :RES], values[:, RES:]], axis=0).astype(BF16)

    def put_channel(values, slot):
        pack[pl.ds(slot, DEVICES, stride=8), :] = jnp.concatenate([values[:DEVICES], values[DEVICES:]], axis=1)

    view = right_all.at[:, pl.ds(0, DEVICES - 1)]
    remote(view, view, 0, other).wait_recv()
    spread[...] = mul(
        right_all[...].reshape(RES * OUT, SEQ), left_own[...].reshape(ROWS * OUT, SEQ), NT
    ) * (1.0 / SEQ)
    for b in range(OUT):
        piece = spread[pl.ds(b, RES, stride=OUT), :].astype(BF16)
        for i in range(ROWS):
            outer_mean[i * RES : (i + 1) * RES, b * OUT : (b + 1) * OUT] = piece[:, i * OUT : (i + 1) * OUT]
    pair = pair + mul(outer_mean[...], mean_swapped_ref[...]).T

    pair = pair.astype(BF16).astype(F32)
    for t in range(2):
        normed, inverse = normalize(pair, 0)
        normed_s[t] = normed
        half = normed.astype(BF16)
        projected = mul(triangle_t[t, : 5 * CH], half)
        parts_s[t, 0] = projected[:CH]
        parts_s[t, 1] = jax.nn.sigmoid(projected[CH : 2 * CH])
        parts_s[t, 2] = projected[2 * CH : 3 * CH]
        parts_s[t, 3] = jax.nn.sigmoid(projected[3 * CH : 4 * CH])
        gate_s[t] = jax.nn.sigmoid(projected[4 * CH :])
        put(parts_s[t, 0] * parts_s[t, 1], 0)
        put(parts_s[t, 2] * parts_s[t, 3], PER)
        post(factor_send.at[t])
        exchange(factor_send.at[t], factor_recv.at[t], 2 + t)
        tail_s[t, 2, :1] = inverse
        arrived(factor_recv.at[t], 2 + t)
        take(factor_recv.at[t])
        mixed = []
        for k in range(PER):
            left, right = channel(k), channel(PER + k)
            left_chan[t, k] = left
            right_chan[t, k] = right
            mixed.append(mul(left, right, NT if t == 0 else TN))
        for k in range(PER):
            put_channel(mixed[k], k)
        post(mixed_send.at[t])
        exchange(mixed_send.at[t], mixed_recv.at[t], 4 + t)
        arrived(mixed_recv.at[t], 4 + t)
        take(mixed_recv.at[t])
        mixed_norm, mixed_inverse = normalize(get(0), 0)
        update = mul(triangle_t[t, 5 * CH :], mixed_norm.astype(BF16))
        tail_s[t, 0] = mixed_norm
        tail_s[t, 1] = update
        tail_s[t, 2, 8:9] = mixed_inverse
        pair = (pair + gate_s[t] * update).astype(BF16).astype(F32)
    updated_ref[...] = pair.T.astype(BF16)

    def rows_of(t):
        return (early_send, 0) if t == 1 else (late_send, 0)

    for t in (1, 0):
        upstream = upstream_s[1 - t]
        gate = gate_s[t]
        mixed_norm = tail_s[t, 0]
        update_grad = (upstream * gate).astype(BF16)
        logit_grad = (upstream * tail_s[t, 1] * gate * (1.0 - gate)).astype(BF16)
        logit_s[t] = logit_grad
        mixed_grad = norm_back(mixed_norm, tail_s[t, 2, 8:9], mul(mixing_ref[t], update_grad), 0)
        put(mixed_grad, 0)
        post(back_send.at[t])
        exchange(back_send.at[t], back_recv.at[t], 6 + t)
        mixing_grad = mul(mixed_norm.astype(BF16), update_grad, NT).astype(BF16)
        half = normed_s[t].astype(BF16)
        gating_grad = mul(half, logit_grad, NT).astype(BF16)
        if t == 1:
            early_send[4 * CH : 5 * CH] = gating_grad
            early_send[5 * CH : 6 * CH] = mixing_grad
        else:
            early_send[6 * CH : 7 * CH] = mixing_grad
            late_send[4 * CH : 5 * CH] = gating_grad
            each_peer(
                lambda peer: remote(
                    early_send.at[pl.ds(pl.multiple_of(peer * (EARLY // DEVICES), EARLY // DEVICES), EARLY // DEVICES)],
                    early_recv.at[me], 10, peer,
                ).start()
            )
            early_recv[me] = early_send[pl.ds(pl.multiple_of(me * (EARLY // DEVICES), EARLY // DEVICES), EARLY // DEVICES)]
        arrived(back_recv.at[t], 6 + t)
        take(back_recv.at[t])
        grads = [channel(k) for k in range(PER)]
        for k in range(PER):
            grad, left, right = grads[k], left_chan[t, k], right_chan[t, k]
            if t == 0:
                left_grad, right_grad = mul(grad, right), mul(grad, left, TN)
            else:
                left_grad, right_grad = mul(right, grad, NT), mul(left, grad)
            put_channel(left_grad, k)
            put_channel(right_grad, PER + k)
        post(grad_send.at[t])
        exchange(grad_send.at[t], grad_recv.at[t], 8 + t)
        if t == 0:
            arrived(early_recv, 10)
            total = jnp.sum(early_recv[...].astype(F32), axis=0).astype(BF16)
            early_own[...] = total
            each_peer(lambda peer: remote(early_own, early_all.at[me], 11, peer).start())
            early_all[me] = total
        arrived(grad_recv.at[t], 8 + t)
        take(grad_recv.at[t])
        left_grad, right_grad = get(0), get(PER)
        linear, switch = parts_s[t, 0], parts_s[t, 1]
        one = (left_grad * switch).astype(BF16)
        two = (left_grad * linear * switch * (1.0 - switch)).astype(BF16)
        linear, switch = parts_s[t, 2], parts_s[t, 3]
        three = (right_grad * switch).astype(BF16)
        four = (right_grad * linear * switch * (1.0 - switch)).astype(BF16)
        quarter = jnp.concatenate([one, two, three, four], axis=0)
        normed_grad = mul(triangle_ref[t], quarter) + mul(gating_ref[t], logit_s[t])
        upstream = upstream + norm_back(normed_s[t], tail_s[t, 2, :1], normed_grad, 0)
        if t == 1:
            upstream_s[1] = upstream
        target = early_send if t == 1 else late_send
        project_grad = mul(half, quarter, NT).astype(BF16)
        for q in range(4):
            target[q * CH : (q + 1) * CH] = project_grad[:, q * CH : (q + 1) * CH]

    cells = upstream.T
    pair_grad_ref[...] = cells
    for k in range(4):
        pack[pl.ds(k, DEVICES, stride=8), :] = cells[k * DEVICES : (k + 1) * DEVICES]
    post(cot_send)
    exchange(cot_send, cot_recv, 12)
    own_cot = cells.astype(BF16)
    late_send[5 * CH : 13 * CH] = mul(outer_mean[...], own_cot, TN).astype(BF16)

    def factor_grad(cot, weight, factors):
        wide = (mul(cot, weight, NT) * (1.0 / SEQ)).astype(BF16).astype(F32)
        for b in range(OUT):
            piece = wide[:, b * OUT : (b + 1) * OUT]
            spread[pl.ds(b, RES, stride=OUT), :] = jnp.concatenate([piece[:RES], piece[RES:]], axis=1)
        return mul(spread[...].astype(BF16), factors[...].reshape(RES * OUT, SEQ), TN).astype(BF16)

    left_grad = factor_grad(own_cot, mean_swapped_ref[...], right_all)
    arrived(cot_recv, 12)
    take(cot_recv)
    theirs = [pack[pl.ds(k, DEVICES, stride=8), :] for k in range(4)]
    cot = jnp.concatenate([theirs[0], theirs[2], theirs[1], theirs[3]], axis=0).astype(BF16)
    view = left_all.at[:, pl.ds(0, DEVICES - 1)]
    remote(view, view, 1, other).wait_recv()
    right_grad = factor_grad(cot, mean_ref[...], left_all)

    grads = [
        jnp.concatenate([left_grad[j * OUT : (j + 1) * OUT], right_grad[j * OUT : (j + 1) * OUT]], axis=0)
        for j in range(ROWS)
    ]
    outer_grad = sum(mul(grads[j], aligned[j].astype(BF16)) for j in range(ROWS)).astype(BF16)
    late_send[13 * CH : 13 * CH + 2 * OUT] = outer_grad[:, :CH]
    late_send[13 * CH + 2 * OUT : 14 * CH] = outer_grad[:, CH:]
    share = LATE // DEVICES
    each_peer(
        lambda peer: remote(
            late_send.at[pl.ds(pl.multiple_of(peer * share, share), share)], late_recv.at[me], 13, peer
        ).start()
    )
    late_recv[me] = late_send[pl.ds(pl.multiple_of(me * share, share), share)]
    for j in range(ROWS):
        back = mul(grads[j], outer_ref[...], (((0,), (1,)), ((), ())))
        alignment_grad_ref[j] = norm_back(aligned[j], aligned_inv[j], back, 1)

    arrived(late_recv, 13)
    total = jnp.sum(late_recv[...].astype(F32), axis=0).astype(BF16)
    late_own[...] = total
    each_peer(lambda peer: remote(late_own, late_all.at[me], 14, peer).start())
    late_all[me] = total

    arrived(early_all, 11)
    early = early_all[...].reshape(EARLY, CH)
    for q in range(4):
        triangle_grad_ref[1, :, q * CH : (q + 1) * CH] = early[q * CH : (q + 1) * CH].astype(F32)
    gating_grad_ref[1] = early[4 * CH : 5 * CH].astype(F32)
    mixing_grad_ref[1] = early[5 * CH : 6 * CH].astype(F32)
    mixing_grad_ref[0] = early[6 * CH : 7 * CH].astype(F32)

    for own, phase in ((right_all, 0), (left_all, 1)):
        view = own.at[:, pl.ds(0, DEVICES - 1)]
        remote(view, view, phase, other).wait_send()
    for t in range(2):
        sent(factor_recv.at[t], 2 + t)
        sent(mixed_recv.at[t], 4 + t)
        sent(back_recv.at[t], 6 + t)
        sent(grad_recv.at[t], 8 + t)
    sent(early_recv, 10)
    sent(early_all, 11)
    sent(cot_recv, 12)
    sent(late_recv, 13)

    arrived(late_all, 14)
    late = late_all[...].reshape(LATE, CH)
    for q in range(4):
        triangle_grad_ref[0, :, q * CH : (q + 1) * CH] = late[q * CH : (q + 1) * CH].astype(F32)
    gating_grad_ref[0] = late[4 * CH : 5 * CH].astype(F32)
    mean_grad_ref[...] = late[5 * CH : 13 * CH].astype(F32)
    outer_grad_ref[:, :CH] = late[13 * CH : 13 * CH + 2 * OUT].astype(F32)
    outer_grad_ref[:, CH:] = late[13 * CH + 2 * OUT : 14 * CH].astype(F32)
    sent(late_all, 14)


def on_device(
    alignment, pair_features, pair_cotangent, outer_weight, mean_weight, triangle_weight, gating_weight, mixing_weight
):
    swapped = mean_weight.reshape(OUT, OUT, CH).swapaxes(0, 1).reshape(OUT * OUT, CH)
    message = pltpu.VMEM((2, DEVICES, 8, CELLS), BF16)
    half_early, half_late = EARLY // DEVICES, LATE // DEVICES
    updated, alignment_grad, pair_grad, outer_grad, mean_grad, triangle_grad, gating_grad, mixing_grad = pl.pallas_call(
        kernel,
        out_shape=[
            jax.ShapeDtypeStruct((CELLS, CH), BF16),
            jax.ShapeDtypeStruct((ROWS, SEQ, MSA), F32),
            jax.ShapeDtypeStruct((CELLS, CH), F32),
            jax.ShapeDtypeStruct((2 * OUT, MSA), F32),
            jax.ShapeDtypeStruct((OUT * OUT, CH), F32),
            jax.ShapeDtypeStruct((2, CH, 4 * CH), F32),
            jax.ShapeDtypeStruct((2, CH, CH), F32),
            jax.ShapeDtypeStruct((2, CH, CH), F32),
        ],
        in_specs=[pl.BlockSpec(memory_space=pltpu.VMEM)] * 9,
        out_specs=[pl.BlockSpec(memory_space=pltpu.VMEM)] * 8,
        scratch_shapes=[
            pltpu.VMEM((ROWS, OUT, SEQ), BF16),
            pltpu.VMEM((ROWS, OUT, SEQ), BF16),
            pltpu.VMEM((ROWS, DEVICES, OUT, SEQ), BF16),
            pltpu.VMEM((ROWS, DEVICES, OUT, SEQ), BF16),
            pltpu.VMEM((ROWS, SEQ, MSA), F32),
            pltpu.VMEM((ROWS, SEQ, 1), F32),
            pltpu.VMEM((RES * OUT, ROWS * OUT), F32),
            pltpu.VMEM((CELLS, OUT * OUT), BF16),
            pltpu.VMEM((DEVICES * 8, CELLS), F32),
            message, message, message, message, message, message, message, message,
            pltpu.VMEM((DEVICES, 8, CELLS), BF16),
            pltpu.VMEM((DEVICES, 8, CELLS), BF16),
            pltpu.VMEM((2, PER, RES, RES), BF16),
            pltpu.VMEM((2, PER, RES, RES), BF16),
            pltpu.VMEM((2, 6 * CH, CH), BF16),
            pltpu.VMEM((2, CH, CELLS), F32),
            pltpu.VMEM((2, 4, CH, CELLS), F32),
            pltpu.VMEM((2, CH, CELLS), F32),
            pltpu.VMEM((2, 3, CH, CELLS), F32),
            pltpu.VMEM((2, CH, CELLS), BF16),
            pltpu.VMEM((2, CH, CELLS), F32),
            pltpu.VMEM((EARLY, CH), BF16),
            pltpu.VMEM((DEVICES, half_early, CH), BF16),
            pltpu.VMEM((half_early, CH), BF16),
            pltpu.VMEM((DEVICES, half_early, CH), BF16),
            pltpu.VMEM((LATE, CH), BF16),
            pltpu.VMEM((DEVICES, half_late, CH), BF16),
            pltpu.VMEM((half_late, CH), BF16),
            pltpu.VMEM((DEVICES, half_late, CH), BF16),
            pltpu.SemaphoreType.DMA((15,)),
            pltpu.SemaphoreType.DMA((15,)),
        ],
        compiler_params=pltpu.CompilerParams(
            collective_id=0, has_side_effects=True, vmem_limit_bytes=40 * 1024 * 1024
        ),
        name="evoformer",
    )(
        alignment.swapaxes(0, 1),
        pair_features.reshape(CELLS, CH),
        pair_cotangent.reshape(CELLS, CH),
        outer_weight,
        mean_weight,
        swapped,
        triangle_weight,
        gating_weight,
        mixing_weight,
    )

    def natural(values):
        return values.reshape(ROWS, 2, DEVICES, CH).swapaxes(1, 2).reshape(ROWS, RES, CH)

    return (
        natural(updated),
        alignment_grad.swapaxes(0, 1),
        natural(pair_grad),
        outer_grad.T,
        mean_grad.reshape(OUT, OUT, CH).swapaxes(0, 1).reshape(OUT * OUT, CH),
        triangle_grad,
        gating_grad,
        mixing_grad,
    )


def solution(mesh):
    in_specs = (
        P("crop", "res", None),
        P("res", "crop", None),
        P("res", "crop", None),
        P(),
        P(),
        P(),
        P(),
        P(),
    )
    out_specs = (
        P("res", "crop", None),
        P("crop", "res", None),
        P("res", "crop", None),
        P("crop", None),
        P("crop", None),
        P("crop", None, None),
        P("crop", None, None),
        P("crop", None, None),
    )
    return jax.shard_map(
        on_device, mesh=mesh, in_specs=in_specs, out_specs=out_specs, check_vma=False
    )
```

```python
import functools

import jax
import jax.numpy as jnp
from jax import lax
from jax.experimental import pallas as pl
from jax.experimental.pallas import tpu as pltpu
from jax.sharding import PartitionSpec as P

EPS = 1e-05
F32 = jnp.float32
BF16 = jnp.bfloat16
MESH = pl.DeviceIdType.MESH

DEVICES = 32
ROWS = 2
RES = DEVICES * ROWS
CELLS = ROWS * RES
CH = 128
OUT = 32
SEQ = 128
MSA = 256
PER = CH // DEVICES
EARLY = 32
LATE = 48
CHIPS = 16
FAR = ((2, 1), (2, 0), (1, 1), (3, 1), (1, 0), (3, 0), (0, 1))
GRID = (4, 4, 2)


NN = (((1,), (0,)), ((), ()))
NT = (((1,), (1,)), ((), ()))
TN = (((0,), (0,)), ((), ()))


def mul(a, b, dims=NN):
    return lax.dot_general(a, b, dims, preferred_element_type=F32)


def normalize(values, axis):
    shifted = values - jnp.mean(values, axis=axis, keepdims=True)
    inverse = lax.rsqrt(jnp.mean(shifted * shifted, axis=axis, keepdims=True) + EPS)
    return shifted * inverse, inverse


def norm_back(normed, inverse, upstream, axis):
    mean_upstream = jnp.mean(upstream, axis=axis, keepdims=True)
    mean_product = jnp.mean(upstream * normed, axis=axis, keepdims=True)
    return inverse * (upstream - mean_upstream - normed * mean_product)


def kernel(
    alignment_ref, pair_ref, cotangent_ref, outer_ref, mean_ref, mean_swapped_ref, triangle_ref, gating_ref, mixing_ref,
    updated_ref, alignment_grad_ref, pair_grad_ref, outer_grad_ref, mean_grad_ref, triangle_grad_ref, gating_grad_ref,
    mixing_grad_ref,
    left_own, right_own, left_all, right_all, aligned, aligned_inv, spread, outer_mean, pack,
    factor_send, factor_recv, mixed_send, mixed_recv, back_send, back_recv, grad_send, grad_recv, cot_send, cot_recv,
    outer_send, outer_recv, outer_own, outer_all,
    left_chan, right_chan, triangle_t, normed_s, parts_s, gate_s, tail_s, logit_s, upstream_s,
    early_send, early_near, early_class, early_far, early_own, early_all,
    late_send, late_near, late_class, late_far, late_own, late_all,
    send_sem, recv_sem,
):
    me = lax.axis_index("res")
    other = lax.rem(me + 1, DEVICES)
    z, x = me // 2, lax.rem(me, 2)
    group, kind = z // 4, lax.rem(z, 4)

    def each_peer(body):
        body(lax.rem(me + DEVICES // 2, DEVICES))

        def step(k, carry):
            body(lax.rem(me + DEVICES // 2 + k, DEVICES))
            body(lax.rem(me + DEVICES // 2 - k, DEVICES))
            return carry

        lax.fori_loop(1, DEVICES // 2, step, 0)

    def remote(source, target, phase, peer):
        return pltpu.make_async_remote_copy(
            src_ref=source, dst_ref=target, send_sem=send_sem.at[phase], recv_sem=recv_sem.at[phase],
            device_id={"res": peer}, device_id_type=MESH,
        )

    def received(view, phase):
        remote(view, view, phase, other).wait_recv()

    def left(view, phase):
        remote(view, view, phase, other).wait_send()

    def exchange(send, recv, phase):
        each_peer(lambda peer: remote(send.at[peer], recv.at[me], phase, peer).start())
        recv[me] = send[me]

    def arrived(recv, phase):
        received(recv.at[pl.ds(0, DEVICES - 1)], phase)

    def sent(recv, phase):
        left(recv.at[pl.ds(0, DEVICES - 1)], phase)

    far_place = [(lax.rem(group + m, 4), 1 - x if flip else x) for m, flip in FAR]
    far_peer = [(4 * g + kind) * 2 + xx for g, xx in far_place]
    far_source = [(lax.rem(group + 4 - m, 4), 1 - x if flip else x) for m, flip in FAR]
    near_kind = [lax.rem(kind + n, 4) for n in (1, 3, 2)]
    near_peer = [lax.rem(z + step, CHIPS) * 2 + x for step in (1, CHIPS - 1, CHIPS + 2 - 4 * (kind // 2))]

    def gather_far(own, whole, phase):
        for k in range(len(FAR)):
            remote(own, whole(group, kind, x), phase + k, far_peer[k]).start()

    def gather_near(whole, phase):
        for n in range(3):
            remote(whole(slice(None), kind, slice(None)), whole(slice(None), kind, slice(None)), phase, near_peer[n]).start()

    def forward_block(whole, g, xx, phase):
        for n in range(3):
            remote(whole(g, kind, xx), whole(g, kind, xx), phase, near_peer[n]).start()

    def gather_forward(whole, far_phase, phase):
        forward_block(whole, group, x, phase)
        for k in reversed(range(len(FAR))):
            g, xx = far_source[k]
            received(whole(g, kind, xx), far_phase + k)
            forward_block(whole, g, xx, phase)

    def far_received(whole, phase):
        for k, (g, xx) in enumerate(far_source):
            received(whole(g, kind, xx), phase + k)

    def gather_left(whole, far_phase, phase):
        for k, (g, xx) in enumerate(far_source):
            left(whole(g, kind, xx), far_phase + k)
        left(whole(slice(None), pl.ds(0, 3), slice(None)), phase)

    def near_received(whole, phase):
        received(whole(slice(None), pl.ds(0, 3), slice(None)), phase)

    def scatter_near(send, near, phase):
        for n in range(3):
            remote(send.at[:, near_kind[n]], near.at[n], phase, near_peer[n]).start()

    def scatter_far(send, near, of_class, far, near_phase, phase):
        received(near, near_phase)
        of_class[...] = (send[:, kind].astype(F32) + jnp.sum(near[...].astype(F32), axis=0)).astype(BF16)
        for k, (g, xx) in enumerate(far_place):
            remote(of_class.at[g, xx], far.at[k + 1], phase, far_peer[k]).start()
        far[0] = of_class[group, x]

    def scatter_sum(far, own, whole, phase):
        received(far.at[pl.ds(1, 7)], phase)
        total = jnp.sum(far[...].astype(F32), axis=0).astype(BF16)
        own[...] = total
        whole[group, kind, x] = total

    def scatter_left(near, far, near_phase, phase):
        left(near, near_phase)
        left(far.at[pl.ds(1, 7)], phase)

    rights = lambda g, k, xx: right_all.at[:, g, k, xx]
    lefts = lambda g, k, xx: left_all.at[:, g, k, xx]
    earlies = lambda g, k, xx: early_all.at[g, k, xx]
    lates = lambda g, k, xx: late_all.at[g, k, xx]

    barrier = pltpu.get_barrier_semaphore()
    each_peer(lambda peer: pl.semaphore_signal(barrier, inc=1, device_id={"res": peer}, device_id_type=MESH))

    for j in range(ROWS):
        normed, inverse = normalize(alignment_ref[j].astype(F32), 1)
        aligned[j] = normed
        aligned_inv[j] = inverse
        projected = mul(outer_ref[...], normed.astype(BF16), (((0,), (1,)), ((), ()))).astype(BF16)
        left_own[j] = projected[:OUT]
        right_own[j] = projected[OUT:]
    pl.semaphore_wait(barrier, DEVICES - 1)

    gather_far(right_own, rights, 20)
    right_all[:, group, kind, x] = right_own[...]
    left_all[:, group, kind, x] = left_own[...]

    row = lax.broadcasted_iota(jnp.int32, (CELLS, CELLS), 0)
    column = lax.broadcasted_iota(jnp.int32, (CELLS, CELLS), 1)
    place = (row // RES) * RES + lax.rem(row, 2) * DEVICES + lax.rem(row, RES) // 2
    order = jnp.where(place == column, 1.0, 0.0).astype(BF16)
    pair = mul(pair_ref[...], order, TN)
    upstream_s[0] = mul(cotangent_ref[...], order, TN)
    for t in range(2):
        triangle_t[t, : 4 * CH] = triangle_ref[t].T
        triangle_t[t, 4 * CH : 5 * CH] = gating_ref[t].T
        triangle_t[t, 5 * CH :] = mixing_ref[t].T
    pack[...] = jnp.zeros_like(pack)
    gather_forward(rights, 20, 0)

    def put(values, slot):
        for k in range(PER):
            pack[pl.ds(slot + k, DEVICES, stride=8), :] = values[k * DEVICES : (k + 1) * DEVICES]

    def post(send):
        send[...] = pack[...].reshape(DEVICES, 8, CELLS).astype(BF16)

    def take(recv):
        pack[...] = recv[...].astype(F32).reshape(DEVICES * 8, CELLS)

    def get(slot):
        return jnp.concatenate([pack[pl.ds(slot + k, DEVICES, stride=8), :] for k in range(PER)], axis=0)

    def channel(slot):
        values = pack[pl.ds(slot, DEVICES, stride=8), :]
        return jnp.concatenate([values[:, :RES], values[:, RES:]], axis=0).astype(BF16)

    def put_channel(values, slot):
        pack[pl.ds(slot, DEVICES, stride=8), :] = jnp.concatenate([values[:DEVICES], values[DEVICES:]], axis=1)

    near_received(rights, 0)
    spread[...] = mul(
        right_all[...].reshape(RES * OUT, SEQ), left_own[...].reshape(ROWS * OUT, SEQ), NT
    ) * (1.0 / SEQ)
    for b in range(OUT):
        piece = spread[pl.ds(b, RES, stride=OUT), :].astype(BF16)
        for i in range(ROWS):
            outer_mean[i * RES : (i + 1) * RES, b * OUT : (b + 1) * OUT] = piece[:, i * OUT : (i + 1) * OUT]
    pair = pair + mul(outer_mean[...], mean_swapped_ref[...]).T

    pair = pair.astype(BF16).astype(F32)
    for t in range(2):
        normed, inverse = normalize(pair, 0)
        normed_s[t] = normed
        half = normed.astype(BF16)
        projected = mul(triangle_t[t, : 5 * CH], half)
        parts_s[t, 0] = projected[:CH]
        parts_s[t, 1] = jax.nn.sigmoid(projected[CH : 2 * CH])
        parts_s[t, 2] = projected[2 * CH : 3 * CH]
        parts_s[t, 3] = jax.nn.sigmoid(projected[3 * CH : 4 * CH])
        gate_s[t] = jax.nn.sigmoid(projected[4 * CH :])
        put(parts_s[t, 0] * parts_s[t, 1], 0)
        put(parts_s[t, 2] * parts_s[t, 3], PER)
        post(factor_send.at[t])
        exchange(factor_send.at[t], factor_recv.at[t], 2 + t)
        tail_s[t, 2, :1] = inverse
        if t == 0:
            gather_far(left_own, lefts, 27)
        arrived(factor_recv.at[t], 2 + t)
        take(factor_recv.at[t])
        mixed = []
        for k in range(PER):
            left_k, right_k = channel(k), channel(PER + k)
            left_chan[t, k] = left_k
            right_chan[t, k] = right_k
            mixed.append(mul(left_k, right_k, NT if t == 0 else TN))
        for k in range(PER):
            put_channel(mixed[k], k)
        post(mixed_send.at[t])
        exchange(mixed_send.at[t], mixed_recv.at[t], 4 + t)
        if t == 0:
            far_received(lefts, 27)
            gather_near(lefts, 1)
        arrived(mixed_recv.at[t], 4 + t)
        take(mixed_recv.at[t])
        mixed_norm, mixed_inverse = normalize(get(0), 0)
        update = mul(triangle_t[t, 5 * CH :], mixed_norm.astype(BF16))
        tail_s[t, 0] = mixed_norm
        tail_s[t, 1] = update
        tail_s[t, 2, 8:9] = mixed_inverse
        pair = (pair + gate_s[t] * update).astype(BF16).astype(F32)
    updated_ref[...] = pair.T.astype(BF16)

    early = []
    for t in (1, 0):
        upstream = upstream_s[1 - t]
        gate = gate_s[t]
        mixed_norm = tail_s[t, 0]
        update_grad = (upstream * gate).astype(BF16)
        logit_grad = (upstream * tail_s[t, 1] * gate * (1.0 - gate)).astype(BF16)
        logit_s[t] = logit_grad
        mixed_grad = norm_back(mixed_norm, tail_s[t, 2, 8:9], mul(mixing_ref[t], update_grad), 0)
        put(mixed_grad, 0)
        post(back_send.at[t])
        exchange(back_send.at[t], back_recv.at[t], 6 + t)
        mixing_grad = mul(mixed_norm.astype(BF16), update_grad, NT).astype(BF16)
        half = normed_s[t].astype(BF16)
        gating_grad = mul(half, logit_grad, NT).astype(BF16)
        early += [gating_grad, mixing_grad]
        if t == 0:
            early_send[...] = jnp.concatenate(early, axis=0).reshape(GRID + (EARLY, CH))
            scatter_near(early_send, early_near, 13)
        arrived(back_recv.at[t], 6 + t)
        take(back_recv.at[t])
        grads = [channel(k) for k in range(PER)]
        for k in range(PER):
            grad, left_k, right_k = grads[k], left_chan[t, k], right_chan[t, k]
            if t == 0:
                left_grad, right_grad = mul(grad, right_k), mul(grad, left_k, TN)
            else:
                left_grad, right_grad = mul(right_k, grad, NT), mul(left_k, grad)
            put_channel(left_grad, k)
            put_channel(right_grad, PER + k)
        post(grad_send.at[t])
        exchange(grad_send.at[t], grad_recv.at[t], 8 + t)
        if t == 0:
            scatter_far(early_send, early_near, early_class, early_far, 13, 14)
        arrived(grad_recv.at[t], 8 + t)
        take(grad_recv.at[t])
        left_grad, right_grad = get(0), get(PER)
        linear, switch = parts_s[t, 0], parts_s[t, 1]
        one = (left_grad * switch).astype(BF16)
        two = (left_grad * linear * switch * (1.0 - switch)).astype(BF16)
        linear, switch = parts_s[t, 2], parts_s[t, 3]
        three = (right_grad * switch).astype(BF16)
        four = (right_grad * linear * switch * (1.0 - switch)).astype(BF16)
        quarter = jnp.concatenate([one, two, three, four], axis=0)
        normed_grad = mul(triangle_ref[t], quarter) + mul(gating_ref[t], logit_s[t])
        upstream = upstream + norm_back(normed_s[t], tail_s[t, 2, :1], normed_grad, 0)
        if t == 1:
            upstream_s[1] = upstream
        project_grad = mul(half, quarter, NT).astype(BF16)
        pieces = [project_grad[:, q * CH : (q + 1) * CH] for q in range(4)]
        if t == 1:
            early += pieces
        else:
            late = pieces

    cells = upstream.T
    pair_grad_ref[...] = cells
    for k in range(4):
        pack[pl.ds(k, DEVICES, stride=8), :] = cells[k * DEVICES : (k + 1) * DEVICES]
    post(cot_send)
    exchange(cot_send, cot_recv, 10)
    own_cot = cells.astype(BF16)
    late.append(mul(outer_mean[...], own_cot, TN).astype(BF16))
    late_send[...] = jnp.concatenate(late, axis=0).reshape(GRID + (LATE, CH))
    scatter_near(late_send, late_near, 16)
    scatter_sum(early_far, early_own, early_all, 14)
    gather_far(early_own, earlies, 34)

    def factor_grad(cot, weight, factors):
        wide = (mul(cot, weight, NT) * (1.0 / SEQ)).astype(BF16).astype(F32)
        for b in range(OUT):
            piece = wide[:, b * OUT : (b + 1) * OUT]
            spread[pl.ds(b, RES, stride=OUT), :] = jnp.concatenate([piece[:RES], piece[RES:]], axis=1)
        return mul(spread[...].astype(BF16), factors[...].reshape(RES * OUT, SEQ), TN).astype(BF16)

    left_grad = factor_grad(own_cot, mean_swapped_ref[...], right_all)
    scatter_far(late_send, late_near, late_class, late_far, 16, 17)
    arrived(cot_recv, 10)
    take(cot_recv)
    theirs = [pack[pl.ds(k, DEVICES, stride=8), :] for k in range(4)]
    cot = jnp.concatenate([theirs[0], theirs[2], theirs[1], theirs[3]], axis=0).astype(BF16)
    near_received(lefts, 1)
    right_grad = factor_grad(cot, mean_ref[...], left_all)

    grads = [
        jnp.concatenate([left_grad[j * OUT : (j + 1) * OUT], right_grad[j * OUT : (j + 1) * OUT]], axis=0)
        for j in range(ROWS)
    ]
    outer_grad = sum(mul(grads[j], aligned[j].astype(BF16)) for j in range(ROWS))
    put(jnp.concatenate([outer_grad[:, :CH], outer_grad[:, CH:]], axis=0), 0)
    post(outer_send)
    exchange(outer_send, outer_recv, 11)
    far_received(earlies, 34)
    gather_near(earlies, 15)
    for j in range(ROWS):
        back = mul(grads[j], outer_ref[...], (((0,), (1,)), ((), ())))
        alignment_grad_ref[j] = norm_back(aligned[j], aligned_inv[j], back, 1)

    scatter_sum(late_far, late_own, late_all, 17)
    gather_far(late_own, lates, 41)
    arrived(outer_recv, 11)
    total = jnp.sum(outer_recv[...].astype(F32), axis=0).astype(BF16)
    outer_own[...] = total
    each_peer(lambda peer: remote(outer_own, outer_all.at[me], 12, peer).start())
    outer_all[me] = total
    gather_forward(lates, 41, 18)

    near_received(earlies, 15)
    early = early_all[...].reshape(DEVICES * EARLY, CH)
    gating_grad_ref[1] = early[:CH].astype(F32)
    mixing_grad_ref[1] = early[CH : 2 * CH].astype(F32)
    for q in range(4):
        triangle_grad_ref[1, :, q * CH : (q + 1) * CH] = early[(2 + q) * CH : (3 + q) * CH].astype(F32)
    gating_grad_ref[0] = early[6 * CH : 7 * CH].astype(F32)
    mixing_grad_ref[0] = early[7 * CH :].astype(F32)

    gather_left(rights, 20, 0)
    gather_left(lefts, 27, 1)
    for t in range(2):
        sent(factor_recv.at[t], 2 + t)
        sent(mixed_recv.at[t], 4 + t)
        sent(back_recv.at[t], 6 + t)
        sent(grad_recv.at[t], 8 + t)
    sent(cot_recv, 10)
    sent(outer_recv, 11)
    sent(outer_all, 12)
    scatter_left(early_near, early_far, 13, 14)
    gather_left(earlies, 34, 15)
    scatter_left(late_near, late_far, 16, 17)

    arrived(outer_all, 12)
    take(outer_all)
    outer = get(0)
    outer_grad_ref[:, :CH] = outer[: 2 * OUT]
    outer_grad_ref[:, CH:] = outer[2 * OUT :]
    near_received(lates, 18)
    late = late_all[...].reshape(DEVICES * LATE, CH)
    for q in range(4):
        triangle_grad_ref[0, :, q * CH : (q + 1) * CH] = late[q * CH : (q + 1) * CH].astype(F32)
    mean_grad_ref[...] = late[4 * CH :].astype(F32)
    gather_left(lates, 41, 18)


def on_device(
    alignment, pair_features, pair_cotangent, outer_weight, mean_weight, triangle_weight, gating_weight, mixing_weight
):
    swapped = mean_weight.reshape(OUT, OUT, CH).swapaxes(0, 1).reshape(OUT * OUT, CH)

    def sums(rows):
        shapes = (GRID, (3, 4, 2), (4, 2), (8,), (), GRID)
        return [pltpu.VMEM(shape + (rows, CH), BF16) for shape in shapes]

    message = pltpu.VMEM((2, DEVICES, 8, CELLS), BF16)
    updated, alignment_grad, pair_grad, outer_grad, mean_grad, triangle_grad, gating_grad, mixing_grad = pl.pallas_call(
        kernel,
        out_shape=[
            jax.ShapeDtypeStruct((CELLS, CH), BF16),
            jax.ShapeDtypeStruct((ROWS, SEQ, MSA), F32),
            jax.ShapeDtypeStruct((CELLS, CH), F32),
            jax.ShapeDtypeStruct((2 * OUT, MSA), F32),
            jax.ShapeDtypeStruct((OUT * OUT, CH), F32),
            jax.ShapeDtypeStruct((2, CH, 4 * CH), F32),
            jax.ShapeDtypeStruct((2, CH, CH), F32),
            jax.ShapeDtypeStruct((2, CH, CH), F32),
        ],
        in_specs=[pl.BlockSpec(memory_space=pltpu.VMEM)] * 9,
        out_specs=[pl.BlockSpec(memory_space=pltpu.VMEM)] * 8,
        scratch_shapes=[
            pltpu.VMEM((ROWS, OUT, SEQ), BF16),
            pltpu.VMEM((ROWS, OUT, SEQ), BF16),
            pltpu.VMEM((ROWS,) + GRID + (OUT, SEQ), BF16),
            pltpu.VMEM((ROWS,) + GRID + (OUT, SEQ), BF16),
            pltpu.VMEM((ROWS, SEQ, MSA), F32),
            pltpu.VMEM((ROWS, SEQ, 1), F32),
            pltpu.VMEM((RES * OUT, ROWS * OUT), F32),
            pltpu.VMEM((CELLS, OUT * OUT), BF16),
            pltpu.VMEM((DEVICES * 8, CELLS), F32),
            message, message, message, message, message, message, message, message,
            pltpu.VMEM((DEVICES, 8, CELLS), BF16),
            pltpu.VMEM((DEVICES, 8, CELLS), BF16),
            pltpu.VMEM((DEVICES, 8, CELLS), BF16),
            pltpu.VMEM((DEVICES, 8, CELLS), BF16),
            pltpu.VMEM((8, CELLS), BF16),
            pltpu.VMEM((DEVICES, 8, CELLS), BF16),
            pltpu.VMEM((2, PER, RES, RES), BF16),
            pltpu.VMEM((2, PER, RES, RES), BF16),
            pltpu.VMEM((2, 6 * CH, CH), BF16),
            pltpu.VMEM((2, CH, CELLS), F32),
            pltpu.VMEM((2, 4, CH, CELLS), F32),
            pltpu.VMEM((2, CH, CELLS), F32),
            pltpu.VMEM((2, 3, CH, CELLS), F32),
            pltpu.VMEM((2, CH, CELLS), BF16),
            pltpu.VMEM((2, CH, CELLS), F32),
            *sums(EARLY),
            *sums(LATE),
            pltpu.SemaphoreType.DMA((48,)),
            pltpu.SemaphoreType.DMA((48,)),
        ],
        compiler_params=pltpu.CompilerParams(
            collective_id=0, has_side_effects=True, vmem_limit_bytes=40 * 1024 * 1024
        ),
        name="evoformer",
    )(
        alignment.swapaxes(0, 1),
        pair_features.reshape(CELLS, CH),
        pair_cotangent.reshape(CELLS, CH),
        outer_weight,
        mean_weight,
        swapped,
        triangle_weight,
        gating_weight,
        mixing_weight,
    )

    def natural(values):
        return values.reshape(ROWS, 2, DEVICES, CH).swapaxes(1, 2).reshape(ROWS, RES, CH)

    return (
        natural(updated),
        alignment_grad.swapaxes(0, 1),
        natural(pair_grad),
        outer_grad.T,
        mean_grad.reshape(OUT, OUT, CH).swapaxes(0, 1).reshape(OUT * OUT, CH),
        triangle_grad,
        gating_grad,
        mixing_grad,
    )


def solution(mesh):
    in_specs = (
        P("crop", "res", None),
        P("res", "crop", None),
        P("res", "crop", None),
        P(),
        P(),
        P(),
        P(),
        P(),
    )
    out_specs = (
        P("res", "crop", None),
        P("crop", "res", None),
        P("res", "crop", None),
        P("crop", None),
        P("crop", None),
        P("crop", None, None),
        P("crop", None, None),
        P("crop", None, None),
    )
    return jax.shard_map(
        on_device, mesh=mesh, in_specs=in_specs, out_specs=out_specs, check_vma=False
    )
```

```python
import functools

import jax
import jax.numpy as jnp
from jax import lax
from jax.experimental import pallas as pl
from jax.experimental.pallas import tpu as pltpu
from jax.sharding import PartitionSpec as P

EPS = 1e-05
F32 = jnp.float32
BF16 = jnp.bfloat16
MESH = pl.DeviceIdType.MESH

DEVICES = 32
ROWS = 2
RES = DEVICES * ROWS
CELLS = ROWS * RES
CH = 128
OUT = 32
SEQ = 128
MSA = 256
PER = CH // DEVICES
EARLY = 32
LATE = 48
CHIPS = 16
FAR = (2, 1, 3)
NEAR = ((2, 1), (1, 1), (3, 1), (2, 0), (1, 0), (3, 0), (0, 1))
GRID = (4, 8)

NN = (((1,), (0,)), ((), ()))
NT = (((1,), (1,)), ((), ()))
TN = (((0,), (0,)), ((), ()))


def mul(a, b, dims=NN):
    return lax.dot_general(a, b, dims, preferred_element_type=F32)


def normalize(values, axis):
    shifted = values - jnp.mean(values, axis=axis, keepdims=True)
    inverse = lax.rsqrt(jnp.mean(shifted * shifted, axis=axis, keepdims=True) + EPS)
    return shifted * inverse, inverse


def norm_back(normed, inverse, upstream, axis):
    mean_upstream = jnp.mean(upstream, axis=axis, keepdims=True)
    mean_product = jnp.mean(upstream * normed, axis=axis, keepdims=True)
    return inverse * (upstream - mean_upstream - normed * mean_product)


def kernel(
    alignment_ref, pair_ref, cotangent_ref, outer_ref, mean_ref, mean_swapped_ref, triangle_ref, gating_ref, mixing_ref,
    updated_ref, alignment_grad_ref, pair_grad_ref, outer_grad_ref, early_ref, late_ref,
    left_own, right_own, left_all, right_all, aligned, aligned_inv, spread, outer_mean, pack,
    factor_send, factor_recv, mixed_send, mixed_recv, back_send, back_recv, grad_send, grad_recv, cot_send, cot_recv,
    outer_send, outer_recv, outer_own, outer_all,
    left_chan, right_chan, triangle_t, normed_s, parts_s, gate_s, tail_s, logit_s, upstream_s,
    early_send, early_near, early_class, early_far, early_own, early_all,
    late_send, late_near, late_class, late_far, late_own, late_all,
    send_sem, recv_sem,
):
    me = lax.axis_index("res")
    other = lax.rem(me + 1, DEVICES)
    z, x = me // 2, lax.rem(me, 2)
    group, kind, place = me // 8, lax.rem(z, 4), lax.rem(me, 8)

    def each_peer(body):
        body(lax.rem(me + DEVICES // 2, DEVICES))

        def step(k, carry):
            body(lax.rem(me + DEVICES // 2 + k, DEVICES))
            body(lax.rem(me + DEVICES // 2 - k, DEVICES))
            return carry

        lax.fori_loop(1, DEVICES // 2, step, 0)

    def remote(source, target, phase, peer):
        return pltpu.make_async_remote_copy(
            src_ref=source, dst_ref=target, send_sem=send_sem.at[phase], recv_sem=recv_sem.at[phase],
            device_id={"res": peer}, device_id_type=MESH,
        )

    def received(view, phase):
        remote(view, view, phase, other).wait_recv()

    def left(view, phase):
        remote(view, view, phase, other).wait_send()

    def exchange(send, recv, phase):
        each_peer(lambda peer: remote(send.at[peer], recv.at[me], phase, peer).start())
        recv[me] = send[me]

    def arrived(recv, phase):
        received(recv.at[pl.ds(0, DEVICES - 1)], phase)

    def sent(recv, phase):
        left(recv.at[pl.ds(0, DEVICES - 1)], phase)

    far_group = [lax.rem(group + m, 4) for m in FAR]
    far_source = [lax.rem(group + 4 - m, 4) for m in FAR]
    steps = {0: 0, 1: 1, 3: CHIPS - 1, 2: CHIPS + 2 - 4 * (kind // 2)}
    near_x = [1 - x if flip else x for _, flip in NEAR]
    near_place = [lax.rem(kind + step, 4) * 2 + xx for (step, _), xx in zip(NEAR, near_x)]
    near_peer = [lax.rem(z + steps[step], CHIPS) * 2 + xx for (step, _), xx in zip(NEAR, near_x)]

    def gather_far(own, whole, phase):
        for k, g in enumerate(far_group):
            remote(own, whole(group, place), phase + k, 8 * g + place).start()

    def gather_near(whole, phase):
        for peer in near_peer:
            remote(whole(slice(None), place), whole(slice(None), place), phase, peer).start()

    def forward_block(whole, g, phase):
        for peer in near_peer:
            remote(whole(g, place), whole(g, place), phase, peer).start()

    def gather_forward(whole, far_phase, phase):
        forward_block(whole, group, phase)
        for k in reversed(range(len(FAR))):
            received(whole(far_source[k], place), far_phase + k)
            forward_block(whole, far_source[k], phase)

    def far_received(whole, phase):
        for k, g in enumerate(far_source):
            received(whole(g, place), phase + k)

    def gather_left(whole, far_phase, phase):
        for k, g in enumerate(far_source):
            left(whole(g, place), far_phase + k)
        left(whole(slice(None), pl.ds(0, 7)), phase)

    def near_received(whole, phase):
        received(whole(slice(None), pl.ds(0, 7)), phase)

    def scatter_near(send, near, phase):
        for n, peer in enumerate(near_peer):
            remote(send.at[:, near_place[n]], near.at[n], phase, peer).start()

    def scatter_far(send, near, of_place, far, near_phase, phase):
        received(near, near_phase)
        of_place[...] = (send[:, place].astype(F32) + jnp.sum(near[...].astype(F32), axis=0)).astype(BF16)
        for k, g in enumerate(far_group):
            remote(of_place.at[g], far.at[k + 1], phase, 8 * g + place).start()
        far[0] = of_place[group]

    def scatter_sum(far, own, whole, phase):
        received(far.at[pl.ds(1, 3)], phase)
        total = jnp.sum(far[...].astype(F32), axis=0).astype(BF16)
        own[...] = total
        whole[group, place] = total

    def scatter_left(near, far, near_phase, phase):
        left(near, near_phase)
        left(far.at[pl.ds(1, 3)], phase)

    rights = lambda g, e: right_all.at[:, g, e]
    lefts = lambda g, e: left_all.at[:, g, e]
    earlies = lambda g, e: early_all.at[g, e]
    lates = lambda g, e: late_all.at[g, e]

    barrier = pltpu.get_barrier_semaphore()
    each_peer(lambda peer: pl.semaphore_signal(barrier, inc=1, device_id={"res": peer}, device_id_type=MESH))

    for j in range(ROWS):
        normed, inverse = normalize(alignment_ref[j].astype(F32), 1)
        aligned[j] = normed
        aligned_inv[j] = inverse
        projected = mul(outer_ref[...], normed.astype(BF16), NT).astype(BF16)
        left_own[j] = projected[:OUT]
        right_own[j] = projected[OUT:]
    pl.semaphore_wait(barrier, DEVICES - 1)

    gather_far(right_own, rights, 20)
    right_all[:, group, place] = right_own[...]
    left_all[:, group, place] = left_own[...]

    row = lax.broadcasted_iota(jnp.int32, (CELLS, CELLS), 0)
    column = lax.broadcasted_iota(jnp.int32, (CELLS, CELLS), 1)
    kept = (row // RES) * RES + lax.rem(row, 2) * DEVICES + lax.rem(row, RES) // 2
    order = jnp.where(kept == column, 1.0, 0.0).astype(BF16)
    pair = mul(pair_ref[...], order, TN)
    upstream_s[0] = mul(cotangent_ref[...], order, TN)
    for t in range(2):
        triangle_t[t, : 4 * CH] = triangle_ref[t].T
        triangle_t[t, 4 * CH : 5 * CH] = gating_ref[t].T
        triangle_t[t, 5 * CH :] = mixing_ref[t].T
    pack[...] = jnp.zeros_like(pack)
    gather_forward(rights, 20, 0)

    def put(values, slot):
        for k in range(PER):
            pack[pl.ds(slot + k, DEVICES, stride=8), :] = values[k * DEVICES : (k + 1) * DEVICES]

    def post(send):
        send[...] = pack[...].reshape(DEVICES, 8, CELLS).astype(BF16)

    def take(recv):
        pack[...] = recv[...].astype(F32).reshape(DEVICES * 8, CELLS)

    def get(slot):
        return jnp.concatenate([pack[pl.ds(slot + k, DEVICES, stride=8), :] for k in range(PER)], axis=0)

    def channel(slot):
        values = pack[pl.ds(slot, DEVICES, stride=8), :]
        return jnp.concatenate([values[:, :RES], values[:, RES:]], axis=0).astype(BF16)

    def put_channel(values, slot):
        pack[pl.ds(slot, DEVICES, stride=8), :] = jnp.concatenate([values[:DEVICES], values[DEVICES:]], axis=1)

    near_received(rights, 0)
    spread[...] = mul(
        right_all[...].reshape(RES * OUT, SEQ), left_own[...].reshape(ROWS * OUT, SEQ), NT
    ) * (1.0 / SEQ)
    for b in range(OUT):
        piece = spread[pl.ds(b, RES, stride=OUT), :].astype(BF16)
        for i in range(ROWS):
            outer_mean[i * RES : (i + 1) * RES, b * OUT : (b + 1) * OUT] = piece[:, i * OUT : (i + 1) * OUT]
    pair = pair + mul(outer_mean[...], mean_swapped_ref[...]).T

    pair = pair.astype(BF16).astype(F32)
    for t in range(2):
        normed, inverse = normalize(pair, 0)
        normed_s[t] = normed
        half = normed.astype(BF16)
        projected = mul(triangle_t[t, : 5 * CH], half)
        parts_s[t, 0] = projected[:CH]
        parts_s[t, 1] = jax.nn.sigmoid(projected[CH : 2 * CH])
        parts_s[t, 2] = projected[2 * CH : 3 * CH]
        parts_s[t, 3] = jax.nn.sigmoid(projected[3 * CH : 4 * CH])
        gate_s[t] = jax.nn.sigmoid(projected[4 * CH :])
        put(parts_s[t, 0] * parts_s[t, 1], 0)
        put(parts_s[t, 2] * parts_s[t, 3], PER)
        post(factor_send.at[t])
        exchange(factor_send.at[t], factor_recv.at[t], 2 + t)
        tail_s[t, 2, :1] = inverse
        if t == 0:
            gather_far(left_own, lefts, 27)
        arrived(factor_recv.at[t], 2 + t)
        take(factor_recv.at[t])
        mixed = []
        for k in range(PER):
            left_k, right_k = channel(k), channel(PER + k)
            left_chan[t, k] = left_k
            right_chan[t, k] = right_k
            mixed.append(mul(left_k, right_k, NT if t == 0 else TN))
        for k in range(PER):
            put_channel(mixed[k], k)
        post(mixed_send.at[t])
        exchange(mixed_send.at[t], mixed_recv.at[t], 4 + t)
        if t == 0:
            far_received(lefts, 27)
            gather_near(lefts, 1)
        arrived(mixed_recv.at[t], 4 + t)
        take(mixed_recv.at[t])
        mixed_norm, mixed_inverse = normalize(get(0), 0)
        update = mul(triangle_t[t, 5 * CH :], mixed_norm.astype(BF16))
        tail_s[t, 0] = mixed_norm
        tail_s[t, 1] = update
        tail_s[t, 2, 8:9] = mixed_inverse
        pair = (pair + gate_s[t] * update).astype(BF16).astype(F32)
    updated_ref[...] = mul(order, pair.astype(BF16), NT).astype(BF16)

    early = []
    for t in (1, 0):
        upstream = upstream_s[1 - t]
        gate = gate_s[t]
        mixed_norm = tail_s[t, 0]
        update_grad = (upstream * gate).astype(BF16)
        logit_grad = (upstream * tail_s[t, 1] * gate * (1.0 - gate)).astype(BF16)
        logit_s[t] = logit_grad
        mixed_grad = norm_back(mixed_norm, tail_s[t, 2, 8:9], mul(mixing_ref[t], update_grad), 0)
        put(mixed_grad, 0)
        post(back_send.at[t])
        exchange(back_send.at[t], back_recv.at[t], 6 + t)
        mixing_grad = mul(mixed_norm.astype(BF16), update_grad, NT).astype(BF16)
        half = normed_s[t].astype(BF16)
        gating_grad = mul(half, logit_grad, NT).astype(BF16)
        early += [gating_grad, mixing_grad]
        if t == 0:
            early_send[...] = jnp.concatenate(early, axis=0).reshape(GRID + (EARLY, CH))
            scatter_near(early_send, early_near, 13)
            scatter_far(early_send, early_near, early_class, early_far, 13, 14)
        arrived(back_recv.at[t], 6 + t)
        take(back_recv.at[t])
        grads = [channel(k) for k in range(PER)]
        for k in range(PER):
            grad, left_k, right_k = grads[k], left_chan[t, k], right_chan[t, k]
            if t == 0:
                left_grad, right_grad = mul(grad, right_k), mul(grad, left_k, TN)
            else:
                left_grad, right_grad = mul(right_k, grad, NT), mul(left_k, grad)
            put_channel(left_grad, k)
            put_channel(right_grad, PER + k)
        post(grad_send.at[t])
        exchange(grad_send.at[t], grad_recv.at[t], 8 + t)
        if t == 0:
            scatter_sum(early_far, early_own, early_all, 14)
            gather_far(early_own, earlies, 34)
        arrived(grad_recv.at[t], 8 + t)
        take(grad_recv.at[t])
        left_grad, right_grad = get(0), get(PER)
        linear, switch = parts_s[t, 0], parts_s[t, 1]
        one = (left_grad * switch).astype(BF16)
        two = (left_grad * linear * switch * (1.0 - switch)).astype(BF16)
        linear, switch = parts_s[t, 2], parts_s[t, 3]
        three = (right_grad * switch).astype(BF16)
        four = (right_grad * linear * switch * (1.0 - switch)).astype(BF16)
        quarter = jnp.concatenate([one, two, three, four], axis=0)
        normed_grad = mul(triangle_ref[t], quarter) + mul(gating_ref[t], logit_s[t])
        upstream = upstream + norm_back(normed_s[t], tail_s[t, 2, :1], normed_grad, 0)
        if t == 1:
            upstream_s[1] = upstream
        project_grad = mul(half, quarter, NT).astype(BF16)
        pieces = [project_grad[:, q * CH : (q + 1) * CH] for q in range(4)]
        if t == 1:
            early += pieces
        else:
            late = pieces

    cells = upstream.T
    for k in range(4):
        pair_grad_ref[pl.ds((k // 2) * RES + k % 2, DEVICES, stride=2), :] = cells[k * DEVICES : (k + 1) * DEVICES]
    for k in range(4):
        pack[pl.ds(k, DEVICES, stride=8), :] = cells[k * DEVICES : (k + 1) * DEVICES]
    post(cot_send)
    exchange(cot_send, cot_recv, 10)
    own_cot = cells.astype(BF16)
    late.append(mul(outer_mean[...], own_cot, TN).astype(BF16))
    late_send[...] = jnp.concatenate(late, axis=0).reshape(GRID + (LATE, CH))
    scatter_near(late_send, late_near, 16)

    def factor_grad(cot, weight, factors):
        wide = (mul(cot, weight, NT) * (1.0 / SEQ)).astype(BF16).astype(F32)
        for b in range(OUT):
            piece = wide[:, b * OUT : (b + 1) * OUT]
            spread[pl.ds(b, RES, stride=OUT), :] = jnp.concatenate([piece[:RES], piece[RES:]], axis=1)
        return mul(spread[...].astype(BF16), factors[...].reshape(RES * OUT, SEQ), TN).astype(BF16)

    left_grad = factor_grad(own_cot, mean_swapped_ref[...], right_all)
    far_received(earlies, 34)
    gather_near(earlies, 15)
    scatter_far(late_send, late_near, late_class, late_far, 16, 17)
    arrived(cot_recv, 10)
    take(cot_recv)
    theirs = [pack[pl.ds(k, DEVICES, stride=8), :] for k in range(4)]
    cot = jnp.concatenate([theirs[0], theirs[2], theirs[1], theirs[3]], axis=0).astype(BF16)
    near_received(lefts, 1)
    right_grad = factor_grad(cot, mean_ref[...], left_all)

    grads = [
        jnp.concatenate([left_grad[j * OUT : (j + 1) * OUT], right_grad[j * OUT : (j + 1) * OUT]], axis=0)
        for j in range(ROWS)
    ]
    outer_grad = sum(mul(grads[j], aligned[j].astype(BF16)) for j in range(ROWS))
    put(jnp.concatenate([outer_grad[:, :CH], outer_grad[:, CH:]], axis=0), 0)
    post(outer_send)
    exchange(outer_send, outer_recv, 11)
    for j in range(ROWS):
        back = mul(grads[j], outer_ref[...], TN)
        alignment_grad_ref[j] = norm_back(aligned[j], aligned_inv[j], back, 1)

    scatter_sum(late_far, late_own, late_all, 17)
    gather_far(late_own, lates, 41)
    arrived(outer_recv, 11)
    total = jnp.sum(outer_recv[...].astype(F32), axis=0).astype(BF16)
    outer_own[...] = total
    each_peer(lambda peer: remote(outer_own, outer_all.at[me], 12, peer).start())
    outer_all[me] = total
    gather_forward(lates, 41, 18)

    near_received(earlies, 15)
    early_ref[...] = early_all[...].reshape(DEVICES * EARLY, CH)

    gather_left(rights, 20, 0)
    gather_left(lefts, 27, 1)
    for t in range(2):
        sent(factor_recv.at[t], 2 + t)
        sent(mixed_recv.at[t], 4 + t)
        sent(back_recv.at[t], 6 + t)
        sent(grad_recv.at[t], 8 + t)
    sent(cot_recv, 10)
    sent(outer_recv, 11)
    sent(outer_all, 12)
    scatter_left(early_near, early_far, 13, 14)
    gather_left(earlies, 34, 15)
    scatter_left(late_near, late_far, 16, 17)

    arrived(outer_all, 12)
    take(outer_all)
    outer = get(0)
    outer_grad_ref[:, :CH] = outer[: 2 * OUT]
    outer_grad_ref[:, CH:] = outer[2 * OUT :]
    near_received(lates, 18)
    late_ref[...] = late_all[...].reshape(DEVICES * LATE, CH)
    gather_left(lates, 41, 18)


def finish(
    updated_ref, alignment_ref, pair_ref, outer_ref, early_ref, late_ref,
    updated_out, alignment_out, pair_out, outer_out, mean_out, triangle_out, gating_out, mixing_out,
):
    updated_out[...] = updated_ref[...]
    pair_out[...] = pair_ref[...]
    outer_out[...] = outer_ref[...]
    for j in range(ROWS):
        alignment_out[:, j, :] = alignment_ref[j]

    def early(k):
        return early_ref[k * CH : (k + 1) * CH].astype(F32)

    gating_out[1], mixing_out[1], gating_out[0], mixing_out[0] = early(0), early(1), early(6), early(7)
    for q in range(4):
        triangle_out[1, :, q * CH : (q + 1) * CH] = early(2 + q)
        triangle_out[0, :, q * CH : (q + 1) * CH] = late_ref[q * CH : (q + 1) * CH].astype(F32)
    for b in range(OUT):
        mean_out[pl.ds(b, OUT, stride=OUT), :] = late_ref[4 * CH + b * OUT : 4 * CH + (b + 1) * OUT].astype(F32)


def on_device(
    alignment, pair_features, pair_cotangent, outer_weight, mean_weight, triangle_weight, gating_weight, mixing_weight
):
    swapped = mean_weight.reshape(OUT, OUT, CH).swapaxes(0, 1).reshape(OUT * OUT, CH)

    def sums(rows):
        shapes = (GRID, (7, 4), (4,), (4,), (), GRID)
        return [pltpu.VMEM(shape + (rows, CH), BF16) for shape in shapes]

    message = pltpu.VMEM((2, DEVICES, 8, CELLS), BF16)
    results = pl.pallas_call(
        kernel,
        out_shape=[
            jax.ShapeDtypeStruct((CELLS, CH), BF16),
            jax.ShapeDtypeStruct((ROWS, SEQ, MSA), F32),
            jax.ShapeDtypeStruct((CELLS, CH), F32),
            jax.ShapeDtypeStruct((2 * OUT, MSA), F32),
            jax.ShapeDtypeStruct((DEVICES * EARLY, CH), BF16),
            jax.ShapeDtypeStruct((DEVICES * LATE, CH), BF16),
        ],
        in_specs=[pl.BlockSpec(memory_space=pltpu.VMEM)] * 9,
        out_specs=[pl.BlockSpec(memory_space=pltpu.VMEM)] * 6,
        scratch_shapes=[
            pltpu.VMEM((ROWS, OUT, SEQ), BF16),
            pltpu.VMEM((ROWS, OUT, SEQ), BF16),
            pltpu.VMEM((ROWS,) + GRID + (OUT, SEQ), BF16),
            pltpu.VMEM((ROWS,) + GRID + (OUT, SEQ), BF16),
            pltpu.VMEM((ROWS, SEQ, MSA), F32),
            pltpu.VMEM((ROWS, SEQ, 1), F32),
            pltpu.VMEM((RES * OUT, ROWS * OUT), F32),
            pltpu.VMEM((CELLS, OUT * OUT), BF16),
            pltpu.VMEM((DEVICES * 8, CELLS), F32),
            message, message, message, message, message, message, message, message,
            pltpu.VMEM((DEVICES, 8, CELLS), BF16),
            pltpu.VMEM((DEVICES, 8, CELLS), BF16),
            pltpu.VMEM((DEVICES, 8, CELLS), BF16),
            pltpu.VMEM((DEVICES, 8, CELLS), BF16),
            pltpu.VMEM((8, CELLS), BF16),
            pltpu.VMEM((DEVICES, 8, CELLS), BF16),
            pltpu.VMEM((2, PER, RES, RES), BF16),
            pltpu.VMEM((2, PER, RES, RES), BF16),
            pltpu.VMEM((2, 6 * CH, CH), BF16),
            pltpu.VMEM((2, CH, CELLS), F32),
            pltpu.VMEM((2, 4, CH, CELLS), F32),
            pltpu.VMEM((2, CH, CELLS), F32),
            pltpu.VMEM((2, 3, CH, CELLS), F32),
            pltpu.VMEM((2, CH, CELLS), BF16),
            pltpu.VMEM((2, CH, CELLS), F32),
            *sums(EARLY),
            *sums(LATE),
            pltpu.SemaphoreType.DMA((48,)),
            pltpu.SemaphoreType.DMA((48,)),
        ],
        compiler_params=pltpu.CompilerParams(
            collective_id=0, has_side_effects=True, vmem_limit_bytes=40 * 1024 * 1024
        ),
        name="evoformer",
    )(
        alignment.swapaxes(0, 1),
        pair_features.reshape(CELLS, CH),
        pair_cotangent.reshape(CELLS, CH),
        outer_weight.T,
        mean_weight,
        swapped,
        triangle_weight,
        gating_weight,
        mixing_weight,
    )

    updated, alignment_grad, pair_grad, outer_grad, mean_grad, triangle_grad, gating_grad, mixing_grad = pl.pallas_call(
        finish,
        out_shape=[
            jax.ShapeDtypeStruct((CELLS, CH), BF16),
            jax.ShapeDtypeStruct((SEQ, ROWS, MSA), F32),
            jax.ShapeDtypeStruct((CELLS, CH), F32),
            jax.ShapeDtypeStruct((2 * OUT, MSA), F32),
            jax.ShapeDtypeStruct((OUT * OUT, CH), F32),
            jax.ShapeDtypeStruct((2, CH, 4 * CH), F32),
            jax.ShapeDtypeStruct((2, CH, CH), F32),
            jax.ShapeDtypeStruct((2, CH, CH), F32),
        ],
        in_specs=[pl.BlockSpec(memory_space=pltpu.VMEM)] * 6,
        out_specs=[pl.BlockSpec(memory_space=pltpu.VMEM)] * 8,
        compiler_params=pltpu.CompilerParams(vmem_limit_bytes=24 * 1024 * 1024),
        name="finish",
    )(*results)
    return (
        updated.reshape(ROWS, RES, CH),
        alignment_grad,
        pair_grad.reshape(ROWS, RES, CH),
        outer_grad.T,
        mean_grad,
        triangle_grad,
        gating_grad,
        mixing_grad,
    )


def solution(mesh):
    in_specs = (
        P("crop", "res", None),
        P("res", "crop", None),
        P("res", "crop", None),
        P(),
        P(),
        P(),
        P(),
        P(),
    )
    out_specs = (
        P("res", "crop", None),
        P("crop", "res", None),
        P("res", "crop", None),
        P("crop", None),
        P("crop", None),
        P("crop", None, None),
        P("crop", None, None),
        P("crop", None, None),
    )
    return jax.shard_map(
        on_device, mesh=mesh, in_specs=in_specs, out_specs=out_specs, check_vma=False
    )
```

```python
import functools

import jax
import jax.numpy as jnp
from jax import lax
from jax.experimental import pallas as pl
from jax.experimental.pallas import tpu as pltpu
from jax.sharding import PartitionSpec as P

EPS = 1e-05
F32 = jnp.float32
BF16 = jnp.bfloat16
MESH = pl.DeviceIdType.MESH

DEVICES = 32
ROWS = 2
RES = DEVICES * ROWS
CELLS = ROWS * RES
CH = 128
OUT = 32
SEQ = 128
MSA = 256
PER = CH // 8
EARLY = 32
LATE = 48
CHIPS = 16
FAR = (2, 1, 3)
NEAR = ((2, 1), (1, 1), (3, 1), (2, 0), (1, 0), (3, 0), (0, 1))
GRID = (4, 8)

NN = (((1,), (0,)), ((), ()))
NT = (((1,), (1,)), ((), ()))
TN = (((0,), (0,)), ((), ()))


def mul(a, b, dims=NN):
    return lax.dot_general(a, b, dims, preferred_element_type=F32)


def normalize(values, axis):
    shifted = values - jnp.mean(values, axis=axis, keepdims=True)
    inverse = lax.rsqrt(jnp.mean(shifted * shifted, axis=axis, keepdims=True) + EPS)
    return shifted * inverse, inverse


def norm_back(normed, inverse, upstream, axis):
    mean_upstream = jnp.mean(upstream, axis=axis, keepdims=True)
    mean_product = jnp.mean(upstream * normed, axis=axis, keepdims=True)
    return inverse * (upstream - mean_upstream - normed * mean_product)


def kernel(
    alignment_ref, pair_ref, cotangent_ref, outer_ref, mean_ref, mean_swapped_ref, triangle_ref, gating_ref, mixing_ref,
    updated_ref, alignment_grad_ref, pair_grad_ref, outer_grad_ref, early_ref, late_ref,
    left_own, right_own, left_all, right_all, aligned, aligned_inv, spread, outer_mean, pack,
    wide_a, wide_b, wide_c,
    left0_send, left0_recv, right0_send, right0_recv, mixed0_send, mixed0_recv,
    factor1_send, factor1_recv, mixed1_send, mixed1_recv,
    back1_send, back1_recv, grad1_send, grad1_recv,
    back0_send, back0_recv, left_grad0_send, left_grad0_recv, right_grad0_send, right_grad0_recv,
    cot_send, cot_recv,
    outer_send, outer_near, outer_part, outer_far, outer_own, outer_all,
    left0_chan, right0_chan, left1_chan, right1_chan, triangle_t, normed_s, parts_s, gate_s, tail_s, logit_s, upstream_s,
    early_send, early_near, early_class, early_far, early_own, early_all,
    late_send, late_near, late_class, late_far, late_own, late_all,
    send_sem, recv_sem,
):
    me = lax.axis_index("res")
    other = lax.rem(me + 1, DEVICES)
    z, x = me // 2, lax.rem(me, 2)
    group, kind, place = me // 8, lax.rem(z, 4), lax.rem(me, 8)

    def each_peer(body):
        body(lax.rem(me + DEVICES // 2, DEVICES))

        def step(k, carry):
            body(lax.rem(me + DEVICES // 2 + k, DEVICES))
            body(lax.rem(me + DEVICES // 2 - k, DEVICES))
            return carry

        lax.fori_loop(1, DEVICES // 2, step, 0)

    def remote(source, target, phase, peer):
        return pltpu.make_async_remote_copy(
            src_ref=source, dst_ref=target, send_sem=send_sem.at[phase], recv_sem=recv_sem.at[phase],
            device_id={"res": peer}, device_id_type=MESH,
        )

    def received(view, phase):
        remote(view, view, phase, other).wait_recv()

    def left(view, phase):
        remote(view, view, phase, other).wait_send()

    def exchange(send, recv, phase):
        each_peer(lambda peer: remote(send.at[peer], recv.at[me], phase, peer).start())
        recv[me] = send[me]

    def exchange_global(send, recv, phase):
        each_peer(lambda peer: remote(send.at[lax.rem(peer, 8)], recv.at[me], phase, peer).start())
        recv[me] = send[place]

    def exchange_near(send, recv, phase):
        for n, peer in enumerate(near_peer):
            remote(send.at[near_place[n]], recv.at[place], phase, peer).start()
        recv[place] = send[place]

    def near_arrived(recv, phase):
        received(recv.at[pl.ds(0, 7)], phase)

    def near_sent(recv, phase):
        left(recv.at[pl.ds(0, 7)], phase)

    def arrived(recv, phase):
        received(recv.at[pl.ds(0, DEVICES - 1)], phase)

    def sent(recv, phase):
        left(recv.at[pl.ds(0, DEVICES - 1)], phase)

    far_group = [lax.rem(group + m, 4) for m in FAR]
    far_source = [lax.rem(group + 4 - m, 4) for m in FAR]
    steps = {0: 0, 1: 1, 3: CHIPS - 1, 2: CHIPS + 2 - 4 * (kind // 2)}
    near_x = [1 - x if flip else x for _, flip in NEAR]
    near_place = [lax.rem(kind + step, 4) * 2 + xx for (step, _), xx in zip(NEAR, near_x)]
    near_peer = [lax.rem(z + steps[step], CHIPS) * 2 + xx for (step, _), xx in zip(NEAR, near_x)]

    def gather_far(own, whole, phase):
        for k, g in enumerate(far_group):
            remote(own, whole(group, place), phase + k, 8 * g + place).start()

    def gather_near(whole, phase):
        for peer in near_peer:
            remote(whole(slice(None), place), whole(slice(None), place), phase, peer).start()

    def forward_block(whole, g, phase):
        for peer in near_peer:
            remote(whole(g, place), whole(g, place), phase, peer).start()

    def forward_arrived(whole, k, far_phase, phase):
        received(whole(far_source[k], place), far_phase + k)
        forward_block(whole, far_source[k], phase)

    def gather_forward(whole, far_phase, phase):
        forward_block(whole, group, phase)
        for k in reversed(range(len(FAR))):
            forward_arrived(whole, k, far_phase, phase)

    def far_received(whole, phase):
        for k, g in enumerate(far_source):
            received(whole(g, place), phase + k)

    def gather_left(whole, far_phase, phase):
        for k, g in enumerate(far_source):
            left(whole(g, place), far_phase + k)
        left(whole(slice(None), pl.ds(0, 7)), phase)

    def near_received(whole, phase):
        received(whole(slice(None), pl.ds(0, 7)), phase)

    def scatter_near(send, near, phase):
        for n, peer in enumerate(near_peer):
            remote(send.at[:, near_place[n]], near.at[n], phase, peer).start()

    def scatter_far(send, near, of_place, far, near_phase, phase):
        received(near, near_phase)
        of_place[...] = (send[:, place].astype(F32) + jnp.sum(near[...].astype(F32), axis=0)).astype(BF16)
        for k, g in enumerate(far_group):
            remote(of_place.at[g], far.at[k + 1], phase, 8 * g + place).start()
        far[0] = of_place[group]

    def scatter_sum(far, own, whole, phase):
        received(far.at[pl.ds(1, 3)], phase)
        total = jnp.sum(far[...].astype(F32), axis=0).astype(BF16)
        own[...] = total
        whole[group, place] = total

    def scatter_left(near, far, near_phase, phase):
        left(near, near_phase)
        left(far.at[pl.ds(1, 3)], phase)

    rights = lambda g, e: right_all.at[:, g, e]
    lefts = lambda g, e: left_all.at[:, g, e]
    earlies = lambda g, e: early_all.at[g, e]
    lates = lambda g, e: late_all.at[g, e]

    barrier = pltpu.get_barrier_semaphore()
    each_peer(lambda peer: pl.semaphore_signal(barrier, inc=1, device_id={"res": peer}, device_id_type=MESH))

    for j in range(ROWS):
        normed, inverse = normalize(alignment_ref[j].astype(F32), 1)
        aligned[j] = normed
        aligned_inv[j] = inverse
        projected = mul(outer_ref[...], normed.astype(BF16), NT).astype(BF16)
        left_own[j] = projected[:OUT]
        right_own[j] = projected[OUT:]
    pl.semaphore_wait(barrier, DEVICES - 1)

    gather_far(right_own, rights, 20)
    right_all[:, group, place] = right_own[...]
    left_all[:, group, place] = left_own[...]

    row = lax.broadcasted_iota(jnp.int32, (CELLS, CELLS), 0)
    column = lax.broadcasted_iota(jnp.int32, (CELLS, CELLS), 1)
    kept = (row // RES) * RES + lax.rem(row, 2) * DEVICES + lax.rem(row, RES) // 2
    order = jnp.where(kept == column, 1.0, 0.0).astype(BF16)
    pair = mul(pair_ref[...], order, TN)
    upstream_s[0] = mul(cotangent_ref[...], order, TN)
    for t in range(2):
        triangle_t[t, : 4 * CH] = triangle_ref[t].T
        triangle_t[t, 4 * CH : 5 * CH] = gating_ref[t].T
        triangle_t[t, 5 * CH :] = mixing_ref[t].T
    pack[...] = jnp.zeros_like(pack)
    gather_forward(rights, 20, 0)

    def post(send):
        send[...] = pack[...].reshape(DEVICES, 8, CELLS).astype(BF16)

    def take(recv):
        pack[...] = recv[...].astype(F32).reshape(DEVICES * 8, CELLS)

    def shards(values):
        return values.astype(BF16).reshape(8, PER, CELLS)

    def whole(values):
        return values.reshape(CH, CELLS).astype(F32)

    def open_wide(wide, values, count):
        wide[: count * PER] = values.astype(F32).reshape(count * PER, CELLS)

    def channel(wide, k, count):
        values = wide[pl.ds(k, count, stride=PER), :]
        return jnp.concatenate([values[:, :RES], values[:, RES:]], axis=0).astype(BF16)

    def put_channel(wide, values, k, count):
        wide[pl.ds(k, count, stride=PER), :] = jnp.concatenate([values[:count], values[count:]], axis=1)

    def close_wide(wide, count):
        return wide[: count * PER].reshape(count, PER, CELLS).astype(BF16)

    def sum_groups(recv):
        total = jnp.sum(recv[...].astype(F32).reshape(4, CH, CELLS), axis=0)
        return total

    near_received(rights, 0)
    spread[...] = mul(
        right_all[...].reshape(RES * OUT, SEQ), left_own[...].reshape(ROWS * OUT, SEQ), NT
    ) * (1.0 / SEQ)
    for b in range(OUT):
        piece = spread[pl.ds(b, RES, stride=OUT), :].astype(BF16)
        for i in range(ROWS):
            outer_mean[i * RES : (i + 1) * RES, b * OUT : (b + 1) * OUT] = piece[:, i * OUT : (i + 1) * OUT]
    pair = pair + mul(outer_mean[...], mean_swapped_ref[...]).T

    def head(t, pair):
        normed, inverse = normalize(pair, 0)
        normed_s[t] = normed
        tail_s[t, 2, :1] = inverse
        projected = mul(triangle_t[t, : 4 * CH], normed.astype(BF16))
        parts_s[t, 0] = projected[:CH]
        parts_s[t, 1] = jax.nn.sigmoid(projected[CH : 2 * CH])
        parts_s[t, 2] = projected[2 * CH : 3 * CH]
        parts_s[t, 3] = jax.nn.sigmoid(projected[3 * CH : 4 * CH])
        return shards(parts_s[t, 0] * parts_s[t, 1]), shards(parts_s[t, 2] * parts_s[t, 3])

    def gate(t):
        gate_s[t] = jax.nn.sigmoid(mul(triangle_t[t, 4 * CH : 5 * CH], normed_s[t].astype(BF16)))

    def tail(t, pair, mixed):
        mixed_norm, mixed_inverse = normalize(mixed, 0)
        update = mul(triangle_t[t, 5 * CH :], mixed_norm.astype(BF16))
        tail_s[t, 0] = mixed_norm
        tail_s[t, 1] = update
        tail_s[t, 2, 8:9] = mixed_inverse
        return (pair + gate_s[t] * update).astype(BF16).astype(F32)

    pair = pair.astype(BF16).astype(F32)
    left_factor, right_factor = head(0, pair)
    right0_send[...] = right_factor
    exchange_global(right0_send, right0_recv, 2)
    left0_send[...] = left_factor
    exchange_near(left0_send, left0_recv, 3)
    gate(0)
    near_arrived(left0_recv, 3)
    open_wide(wide_a, left0_recv[...], 8)
    for k in range(PER):
        left0_chan[k] = channel(wide_a, k, 8)
    arrived(right0_recv, 2)
    open_wide(wide_b, right0_recv[...], DEVICES)
    for k in range(PER):
        right_k = channel(wide_b, k, DEVICES)
        right0_chan[k] = right_k
        put_channel(wide_c, mul(left0_chan[k], right_k, NT), k, 8)
    mixed0_send[...] = close_wide(wide_c, 8)
    exchange_near(mixed0_send, mixed0_recv, 4)
    gather_far(left_own, lefts, 27)
    near_arrived(mixed0_recv, 4)
    pair = tail(0, pair, whole(mixed0_recv[...]))

    left_factor, right_factor = head(1, pair)
    factor1_send[:, 0] = left_factor
    factor1_send[:, 1] = right_factor
    exchange_near(factor1_send, factor1_recv, 5)
    forward_block(lefts, group, 1)
    gate(1)
    near_arrived(factor1_recv, 5)
    open_wide(wide_a, factor1_recv[:, 0], 8)
    open_wide(wide_b, factor1_recv[:, 1], 8)
    for k in range(PER):
        left_k, right_k = channel(wide_a, k, 8), channel(wide_b, k, 8)
        left1_chan[k] = left_k
        right1_chan[k] = right_k
        put_channel(wide_c, mul(left_k, right_k, TN), k, DEVICES)
    mixed1_send[...] = close_wide(wide_c, DEVICES)
    exchange(mixed1_send, mixed1_recv, 6)
    arrived(mixed1_recv, 6)
    pair = tail(1, pair, sum_groups(mixed1_recv))
    updated_ref[...] = mul(order, pair.astype(BF16), NT).astype(BF16)

    def tail_back(t, upstream):
        gated = gate_s[t]
        mixed_norm = tail_s[t, 0]
        update_grad = (upstream * gated).astype(BF16)
        mixed_grad = norm_back(mixed_norm, tail_s[t, 2, 8:9], mul(mixing_ref[t], update_grad), 0)
        return update_grad, shards(mixed_grad)

    def tail_weights(t, upstream, update_grad):
        gated = gate_s[t]
        logit_grad = (upstream * tail_s[t, 1] * gated * (1.0 - gated)).astype(BF16)
        logit_s[t] = logit_grad
        mixing_grad = mul(tail_s[t, 0].astype(BF16), update_grad, NT).astype(BF16)
        return [mul(normed_s[t].astype(BF16), logit_grad, NT).astype(BF16), mixing_grad]

    def head_back(t, upstream, left_grad, right_grad):
        linear, switch = parts_s[t, 0], parts_s[t, 1]
        one = (left_grad * switch).astype(BF16)
        two = (left_grad * linear * switch * (1.0 - switch)).astype(BF16)
        linear, switch = parts_s[t, 2], parts_s[t, 3]
        three = (right_grad * switch).astype(BF16)
        four = (right_grad * linear * switch * (1.0 - switch)).astype(BF16)
        quarter = jnp.concatenate([one, two, three, four], axis=0)
        normed_grad = mul(triangle_ref[t], quarter) + mul(gating_ref[t], logit_s[t])
        return quarter, upstream + norm_back(normed_s[t], tail_s[t, 2, :1], normed_grad, 0)

    def head_weights(t, quarter):
        project_grad = mul(normed_s[t].astype(BF16), quarter, NT).astype(BF16)
        return [project_grad[:, q * CH : (q + 1) * CH] for q in range(4)]

    upstream = upstream_s[0]
    update_grad, back1_send[...] = tail_back(1, upstream)
    exchange_global(back1_send, back1_recv, 7)
    early = tail_weights(1, upstream, update_grad)
    arrived(back1_recv, 7)
    open_wide(wide_a, back1_recv[...], DEVICES)
    for k in range(PER):
        grad = channel(wide_a, k, DEVICES)
        put_channel(wide_b, mul(right1_chan[k], grad, NT), k, 8)
        put_channel(wide_c, mul(left1_chan[k], grad), k, 8)
    grad1_send[:, 0] = close_wide(wide_b, 8)
    grad1_send[:, 1] = close_wide(wide_c, 8)
    exchange_near(grad1_send, grad1_recv, 8)
    forward_arrived(lefts, 1, 27, 1)
    forward_arrived(lefts, 2, 27, 1)
    near_arrived(grad1_recv, 8)
    quarter, upstream = head_back(1, upstream, whole(grad1_recv[:, 0]), whole(grad1_recv[:, 1]))

    update_grad, back0_send[...] = tail_back(0, upstream)
    exchange_near(back0_send, back0_recv, 9)
    forward_arrived(lefts, 0, 27, 1)
    early += head_weights(1, quarter)
    early += tail_weights(0, upstream, update_grad)
    early_send[...] = jnp.concatenate(early, axis=0).reshape(GRID + (EARLY, CH))
    scatter_near(early_send, early_near, 13)
    near_arrived(back0_recv, 9)
    open_wide(wide_a, back0_recv[...], 8)
    grads = []
    for k in range(PER):
        grads.append(channel(wide_a, k, 8))
        put_channel(wide_b, mul(grads[k], left0_chan[k], TN), k, DEVICES)
    right_grad0_send[...] = close_wide(wide_b, DEVICES)
    exchange(right_grad0_send, right_grad0_recv, 45)
    for k in range(PER):
        put_channel(wide_c, mul(grads[k], right0_chan[k]), k, 8)
    left_grad0_send[...] = close_wide(wide_c, 8)
    exchange_near(left_grad0_send, left_grad0_recv, 44)
    scatter_far(early_send, early_near, early_class, early_far, 13, 14)
    near_arrived(left_grad0_recv, 44)
    arrived(right_grad0_recv, 45)
    quarter, upstream = head_back(0, upstream, whole(left_grad0_recv[...]), sum_groups(right_grad0_recv))

    cells = upstream.T
    own_cot = cells.astype(BF16)
    late = head_weights(0, quarter) + [mul(outer_mean[...], own_cot, TN).astype(BF16)]
    late_send[...] = jnp.concatenate(late, axis=0).reshape(GRID + (LATE, CH))
    scatter_near(late_send, late_near, 16)
    for k in range(4):
        pack[pl.ds(k, DEVICES, stride=8), :] = cells[k * DEVICES : (k + 1) * DEVICES]
    post(cot_send)
    exchange(cot_send, cot_recv, 10)
    for k in range(4):
        pair_grad_ref[pl.ds((k // 2) * RES + k % 2, DEVICES, stride=2), :] = cells[k * DEVICES : (k + 1) * DEVICES]
    scatter_sum(early_far, early_own, early_all, 14)
    gather_far(early_own, earlies, 34)

    def factor_grad(cot, weight, factors):
        wide = (mul(cot, weight, NT) * (1.0 / SEQ)).astype(BF16).astype(F32)
        for b in range(OUT):
            piece = wide[:, b * OUT : (b + 1) * OUT]
            spread[pl.ds(b, RES, stride=OUT), :] = jnp.concatenate([piece[:RES], piece[RES:]], axis=1)
        return mul(spread[...].astype(BF16), factors[...].reshape(RES * OUT, SEQ), TN).astype(BF16)

    left_grad = factor_grad(own_cot, mean_swapped_ref[...], right_all)
    scatter_far(late_send, late_near, late_class, late_far, 16, 17)
    arrived(cot_recv, 10)
    take(cot_recv)
    theirs = [pack[pl.ds(k, DEVICES, stride=8), :] for k in range(4)]
    cot = jnp.concatenate([theirs[0], theirs[2], theirs[1], theirs[3]], axis=0).astype(BF16)
    near_received(lefts, 1)
    right_grad = factor_grad(cot, mean_ref[...], left_all)

    grads = [
        jnp.concatenate([left_grad[j * OUT : (j + 1) * OUT], right_grad[j * OUT : (j + 1) * OUT]], axis=0)
        for j in range(ROWS)
    ]
    outer_grad = sum(mul(grads[j], aligned[j].astype(BF16)) for j in range(ROWS))
    outer_grad = jnp.concatenate([outer_grad[:, :CH], outer_grad[:, CH:]], axis=0)
    outer_send[...] = outer_grad.astype(BF16).reshape(8, 16, CH)
    exchange_near(outer_send, outer_near, 11)
    for j in range(ROWS):
        back = mul(grads[j], outer_ref[...], TN)
        alignment_grad_ref[j] = norm_back(aligned[j], aligned_inv[j], back, 1)

    far_received(earlies, 34)
    gather_near(earlies, 15)
    scatter_sum(late_far, late_own, late_all, 17)
    gather_far(late_own, lates, 41)
    near_arrived(outer_near, 11)
    total = jnp.sum(outer_near[...].astype(F32), axis=0).astype(BF16)
    outer_part[...] = total
    for g in far_group:
        remote(outer_part, outer_far.at[group], 12, 8 * g + place).start()
    outer_far[group] = total
    gather_forward(lates, 41, 18)
    received(outer_far.at[pl.ds(0, 3)], 12)
    total = jnp.sum(outer_far[...].astype(F32), axis=0).astype(BF16)
    outer_own[...] = total
    for peer in near_peer:
        remote(outer_own, outer_all.at[place], 46, peer).start()
    outer_all[place] = total

    near_received(earlies, 15)
    early_ref[...] = early_all[...].reshape(DEVICES * EARLY, CH)

    gather_left(rights, 20, 0)
    gather_left(lefts, 27, 1)
    sent(right0_recv, 2)
    near_sent(left0_recv, 3)
    near_sent(mixed0_recv, 4)
    near_sent(factor1_recv, 5)
    sent(mixed1_recv, 6)
    sent(back1_recv, 7)
    near_sent(grad1_recv, 8)
    near_sent(back0_recv, 9)
    near_sent(left_grad0_recv, 44)
    sent(right_grad0_recv, 45)
    sent(cot_recv, 10)
    near_sent(outer_near, 11)
    left(outer_far.at[pl.ds(0, 3)], 12)
    near_sent(outer_all, 46)
    scatter_left(early_near, early_far, 13, 14)
    gather_left(earlies, 34, 15)
    scatter_left(late_near, late_far, 16, 17)

    near_arrived(outer_all, 46)
    outer = outer_all[...].reshape(CH, CH).astype(F32)
    outer_grad_ref[:, :CH] = outer[: 2 * OUT]
    outer_grad_ref[:, CH:] = outer[2 * OUT :]
    near_received(lates, 18)
    late_ref[...] = late_all[...].reshape(DEVICES * LATE, CH)
    gather_left(lates, 41, 18)


def finish(
    updated_ref, alignment_ref, pair_ref, outer_ref, early_ref, late_ref,
    updated_out, alignment_out, pair_out, outer_out, mean_out, triangle_out, gating_out, mixing_out,
):
    updated_out[...] = updated_ref[...]
    pair_out[...] = pair_ref[...]
    outer_out[...] = outer_ref[...]
    for j in range(ROWS):
        alignment_out[:, j, :] = alignment_ref[j]

    def early(k):
        return early_ref[k * CH : (k + 1) * CH].astype(F32)

    gating_out[1], mixing_out[1], gating_out[0], mixing_out[0] = early(0), early(1), early(6), early(7)
    for q in range(4):
        triangle_out[1, :, q * CH : (q + 1) * CH] = early(2 + q)
        triangle_out[0, :, q * CH : (q + 1) * CH] = late_ref[q * CH : (q + 1) * CH].astype(F32)
    for b in range(OUT):
        mean_out[pl.ds(b, OUT, stride=OUT), :] = late_ref[4 * CH + b * OUT : 4 * CH + (b + 1) * OUT].astype(F32)


def on_device(
    alignment, pair_features, pair_cotangent, outer_weight, mean_weight, triangle_weight, gating_weight, mixing_weight
):
    swapped = mean_weight.reshape(OUT, OUT, CH).swapaxes(0, 1).reshape(OUT * OUT, CH)

    def sums(rows):
        shapes = (GRID, (7, 4), (4,), (4,), (), GRID)
        return [pltpu.VMEM(shape + (rows, CH), BF16) for shape in shapes]

    near = pltpu.VMEM((8, PER, CELLS), BF16)
    near_two = pltpu.VMEM((8, 2, PER, CELLS), BF16)
    all_ = pltpu.VMEM((DEVICES, PER, CELLS), BF16)
    results = pl.pallas_call(
        kernel,
        out_shape=[
            jax.ShapeDtypeStruct((CELLS, CH), BF16),
            jax.ShapeDtypeStruct((ROWS, SEQ, MSA), F32),
            jax.ShapeDtypeStruct((CELLS, CH), F32),
            jax.ShapeDtypeStruct((2 * OUT, MSA), F32),
            jax.ShapeDtypeStruct((DEVICES * EARLY, CH), BF16),
            jax.ShapeDtypeStruct((DEVICES * LATE, CH), BF16),
        ],
        in_specs=[pl.BlockSpec(memory_space=pltpu.VMEM)] * 9,
        out_specs=[pl.BlockSpec(memory_space=pltpu.VMEM)] * 6,
        scratch_shapes=[
            pltpu.VMEM((ROWS, OUT, SEQ), BF16),
            pltpu.VMEM((ROWS, OUT, SEQ), BF16),
            pltpu.VMEM((ROWS,) + GRID + (OUT, SEQ), BF16),
            pltpu.VMEM((ROWS,) + GRID + (OUT, SEQ), BF16),
            pltpu.VMEM((ROWS, SEQ, MSA), F32),
            pltpu.VMEM((ROWS, SEQ, 1), F32),
            pltpu.VMEM((RES * OUT, ROWS * OUT), F32),
            pltpu.VMEM((CELLS, OUT * OUT), BF16),
            pltpu.VMEM((DEVICES * 8, CELLS), F32),
            pltpu.VMEM((DEVICES * PER, CELLS), F32),
            pltpu.VMEM((DEVICES * PER, CELLS), F32),
            pltpu.VMEM((DEVICES * PER, CELLS), F32),
            near, near, near, all_, near, near,
            near_two, near_two, all_, all_,
            near, all_, near_two, near_two,
            near, near, near, near, all_, all_,
            pltpu.VMEM((DEVICES, 8, CELLS), BF16),
            pltpu.VMEM((DEVICES, 8, CELLS), BF16),
            pltpu.VMEM((8, 16, CH), BF16),
            pltpu.VMEM((8, 16, CH), BF16),
            pltpu.VMEM((16, CH), BF16),
            pltpu.VMEM((4, 16, CH), BF16),
            pltpu.VMEM((16, CH), BF16),
            pltpu.VMEM((8, 16, CH), BF16),
            pltpu.VMEM((PER, 16, RES), BF16),
            pltpu.VMEM((PER, RES, RES), BF16),
            pltpu.VMEM((PER, 16, RES), BF16),
            pltpu.VMEM((PER, 16, RES), BF16),
            pltpu.VMEM((2, 6 * CH, CH), BF16),
            pltpu.VMEM((2, CH, CELLS), F32),
            pltpu.VMEM((2, 4, CH, CELLS), F32),
            pltpu.VMEM((2, CH, CELLS), F32),
            pltpu.VMEM((2, 3, CH, CELLS), F32),
            pltpu.VMEM((2, CH, CELLS), BF16),
            pltpu.VMEM((2, CH, CELLS), F32),
            *sums(EARLY),
            *sums(LATE),
            pltpu.SemaphoreType.DMA((48,)),
            pltpu.SemaphoreType.DMA((48,)),
        ],
        compiler_params=pltpu.CompilerParams(
            collective_id=0, has_side_effects=True, vmem_limit_bytes=40 * 1024 * 1024
        ),
        name="evoformer",
    )(
        alignment.swapaxes(0, 1),
        pair_features.reshape(CELLS, CH),
        pair_cotangent.reshape(CELLS, CH),
        outer_weight.T,
        mean_weight,
        swapped,
        triangle_weight,
        gating_weight,
        mixing_weight,
    )

    updated, alignment_grad, pair_grad, outer_grad, mean_grad, triangle_grad, gating_grad, mixing_grad = pl.pallas_call(
        finish,
        out_shape=[
            jax.ShapeDtypeStruct((CELLS, CH), BF16),
            jax.ShapeDtypeStruct((SEQ, ROWS, MSA), F32),
            jax.ShapeDtypeStruct((CELLS, CH), F32),
            jax.ShapeDtypeStruct((2 * OUT, MSA), F32),
            jax.ShapeDtypeStruct((OUT * OUT, CH), F32),
            jax.ShapeDtypeStruct((2, CH, 4 * CH), F32),
            jax.ShapeDtypeStruct((2, CH, CH), F32),
            jax.ShapeDtypeStruct((2, CH, CH), F32),
        ],
        in_specs=[pl.BlockSpec(memory_space=pltpu.VMEM)] * 6,
        out_specs=[pl.BlockSpec(memory_space=pltpu.VMEM)] * 8,
        compiler_params=pltpu.CompilerParams(vmem_limit_bytes=24 * 1024 * 1024),
        name="finish",
    )(*results)
    return (
        updated.reshape(ROWS, RES, CH),
        alignment_grad,
        pair_grad.reshape(ROWS, RES, CH),
        outer_grad.T,
        mean_grad,
        triangle_grad,
        gating_grad,
        mixing_grad,
    )


def solution(mesh):
    in_specs = (
        P("crop", "res", None),
        P("res", "crop", None),
        P("res", "crop", None),
        P(),
        P(),
        P(),
        P(),
        P(),
    )
    out_specs = (
        P("res", "crop", None),
        P("crop", "res", None),
        P("res", "crop", None),
        P("crop", None),
        P("crop", None),
        P("crop", None, None),
        P("crop", None, None),
        P("crop", None, None),
    )
    return jax.shard_map(
        on_device, mesh=mesh, in_specs=in_specs, out_specs=out_specs, check_vma=False
    )
```

```python
import functools

import jax
import jax.numpy as jnp
from jax import lax
from jax.experimental import pallas as pl
from jax.experimental.pallas import tpu as pltpu
from jax.sharding import PartitionSpec as P

EPS = 1e-05
F32 = jnp.float32
BF16 = jnp.bfloat16
MESH = pl.DeviceIdType.MESH

DEVICES = 32
ROWS = 2
RES = DEVICES * ROWS
CELLS = ROWS * RES
CH = 128
OUT = 32
SEQ = 128
MSA = 256
PER = CH // 8
EARLY = 32
LATE = 48
CHIPS = 16
FAR = (2, 1, 3)
NEAR = ((2, 1), (1, 1), (3, 1), (2, 0), (1, 0), (3, 0), (0, 1))
GRID = (4, 8)

NN = (((1,), (0,)), ((), ()))
NT = (((1,), (1,)), ((), ()))
TN = (((0,), (0,)), ((), ()))


def mul(a, b, dims=NN):
    return lax.dot_general(a, b, dims, preferred_element_type=F32)


def normalize(values, axis):
    shifted = values - jnp.mean(values, axis=axis, keepdims=True)
    inverse = lax.rsqrt(jnp.mean(shifted * shifted, axis=axis, keepdims=True) + EPS)
    return shifted * inverse, inverse


def norm_back(normed, inverse, upstream, axis):
    mean_upstream = jnp.mean(upstream, axis=axis, keepdims=True)
    mean_product = jnp.mean(upstream * normed, axis=axis, keepdims=True)
    return inverse * (upstream - mean_upstream - normed * mean_product)


def kernel(
    alignment_ref, pair_ref, cotangent_ref, outer_ref, mean_ref, mean_swapped_ref, triangle_ref, gating_ref, mixing_ref,
    updated_ref, alignment_grad_ref, pair_grad_ref, outer_grad_ref, early_ref, late_ref,
    left_own, right_own, left_all, right_all, aligned, aligned_inv, spread, outer_mean, pack,
    wide_a, wide_b, wide_c,
    left0_send, left0_recv, right0_send, right0_recv, mixed0_send, mixed0_recv,
    factor1_send, factor1_recv, mixed1_send, mixed1_recv,
    back1_send, back1_recv, grad1_send, grad1_recv,
    back0_send, back0_recv, left_grad0_send, left_grad0_recv, right_grad0_send, right_grad0_recv,
    cot_send, cot_recv,
    outer_send, outer_near, outer_part, outer_far, outer_own, outer_all,
    left0_chan, right0_chan, left1_chan, right1_chan, triangle_t, normed_s, parts_s, gate_s, tail_s, logit_s, upstream_s,
    early_send, early_near, early_class, early_far, early_own,
    late_send, late_near, late_class, late_far, late_own, late_all,
    send_sem, recv_sem,
):
    me = lax.axis_index("res")
    other = lax.rem(me + 1, DEVICES)
    z, x = me // 2, lax.rem(me, 2)
    group, kind, place = me // 8, lax.rem(z, 4), lax.rem(me, 8)

    def each_peer(body):
        body(lax.rem(me + DEVICES // 2, DEVICES))

        def step(k, carry):
            body(lax.rem(me + DEVICES // 2 + k, DEVICES))
            body(lax.rem(me + DEVICES // 2 - k, DEVICES))
            return carry

        lax.fori_loop(1, DEVICES // 2, step, 0)

    def remote(source, target, phase, peer):
        return pltpu.make_async_remote_copy(
            src_ref=source, dst_ref=target, send_sem=send_sem.at[phase], recv_sem=recv_sem.at[phase],
            device_id={"res": peer}, device_id_type=MESH,
        )

    def received(view, phase):
        remote(view, view, phase, other).wait_recv()

    def left(view, phase):
        remote(view, view, phase, other).wait_send()

    def exchange(send, recv, phase):
        each_peer(lambda peer: remote(send.at[peer], recv.at[me], phase, peer).start())
        recv[me] = send[me]

    def exchange_global(send, recv, phase):
        each_peer(lambda peer: remote(send.at[lax.rem(peer, 8)], recv.at[me], phase, peer).start())
        recv[me] = send[place]

    def exchange_near(send, recv, phase):
        for n, peer in enumerate(near_peer):
            remote(send.at[near_place[n]], recv.at[place], phase, peer).start()
        recv[place] = send[place]

    def near_arrived(recv, phase):
        received(recv.at[pl.ds(0, 7)], phase)

    def near_sent(recv, phase):
        left(recv.at[pl.ds(0, 7)], phase)

    def arrived(recv, phase):
        received(recv.at[pl.ds(0, DEVICES - 1)], phase)

    def sent(recv, phase):
        left(recv.at[pl.ds(0, DEVICES - 1)], phase)

    far_group = [lax.rem(group + m, 4) for m in FAR]
    far_source = [lax.rem(group + 4 - m, 4) for m in FAR]
    steps = {0: 0, 1: 1, 3: CHIPS - 1, 2: CHIPS + 2 - 4 * (kind // 2)}
    near_x = [1 - x if flip else x for _, flip in NEAR]
    near_place = [lax.rem(kind + step, 4) * 2 + xx for (step, _), xx in zip(NEAR, near_x)]
    near_peer = [lax.rem(z + steps[step], CHIPS) * 2 + xx for (step, _), xx in zip(NEAR, near_x)]

    def gather_far(own, whole, phase):
        for k, g in enumerate(far_group):
            remote(own, whole(group, place), phase + k, 8 * g + place).start()

    def gather_near(whole, phase):
        for peer in near_peer:
            remote(whole(slice(None), place), whole(slice(None), place), phase, peer).start()

    def forward_block(whole, g, phase):
        for peer in near_peer:
            remote(whole(g, place), whole(g, place), phase, peer).start()

    def forward_arrived(whole, k, far_phase, phase):
        received(whole(far_source[k], place), far_phase + k)
        forward_block(whole, far_source[k], phase)

    def gather_forward(whole, far_phase, phase):
        forward_block(whole, group, phase)
        for k in reversed(range(len(FAR))):
            forward_arrived(whole, k, far_phase, phase)

    def far_received(whole, phase):
        for k, g in enumerate(far_source):
            received(whole(g, place), phase + k)

    def gather_left(whole, far_phase, phase):
        for k, g in enumerate(far_source):
            left(whole(g, place), far_phase + k)
        left(whole(slice(None), pl.ds(0, 7)), phase)

    def near_received(whole, phase):
        received(whole(slice(None), pl.ds(0, 7)), phase)

    def scatter_near(send, near, phase):
        for n, peer in enumerate(near_peer):
            remote(send.at[:, near_place[n]], near.at[n], phase, peer).start()

    def scatter_far(send, near, of_place, far, near_phase, phase):
        received(near, near_phase)
        of_place[...] = (send[:, place].astype(F32) + jnp.sum(near[...].astype(F32), axis=0)).astype(BF16)
        for k, g in enumerate(far_group):
            remote(of_place.at[g], far.at[k + 1], phase, 8 * g + place).start()
        far[0] = of_place[group]

    def scatter_sum(far, own, whole, phase):
        received(far.at[pl.ds(1, 3)], phase)
        total = jnp.sum(far[...].astype(F32), axis=0).astype(BF16)
        own[...] = total
        whole[group, place] = total

    def scatter_left(near, far, near_phase, phase):
        left(near, near_phase)
        left(far.at[pl.ds(1, 3)], phase)

    rights = lambda g, e: right_all.at[:, g, e]
    lefts = lambda g, e: left_all.at[:, g, e]
    lates = lambda g, e: late_all.at[g, e]

    barrier = pltpu.get_barrier_semaphore()
    each_peer(lambda peer: pl.semaphore_signal(barrier, inc=1, device_id={"res": peer}, device_id_type=MESH))

    for j in range(ROWS):
        normed, inverse = normalize(alignment_ref[j].astype(F32), 1)
        aligned[j] = normed
        aligned_inv[j] = inverse
        projected = mul(outer_ref[...], normed.astype(BF16), NT).astype(BF16)
        left_own[j] = projected[:OUT]
        right_own[j] = projected[OUT:]
    pl.semaphore_wait(barrier, DEVICES - 1)

    gather_far(right_own, rights, 20)
    right_all[:, group, place] = right_own[...]
    left_all[:, group, place] = left_own[...]

    row = lax.broadcasted_iota(jnp.int32, (CELLS, CELLS), 0)
    column = lax.broadcasted_iota(jnp.int32, (CELLS, CELLS), 1)
    kept = (row // RES) * RES + lax.rem(row, 2) * DEVICES + lax.rem(row, RES) // 2
    order = jnp.where(kept == column, 1.0, 0.0).astype(BF16)
    pair = mul(pair_ref[...], order, TN)
    upstream_s[0] = mul(cotangent_ref[...], order, TN)
    for t in range(2):
        triangle_t[t, : 4 * CH] = triangle_ref[t].T
        triangle_t[t, 4 * CH : 5 * CH] = gating_ref[t].T
        triangle_t[t, 5 * CH :] = mixing_ref[t].T
    pack[...] = jnp.zeros_like(pack)
    gather_forward(rights, 20, 0)

    def post(send):
        send[...] = pack[...].reshape(DEVICES, 8, CELLS).astype(BF16)

    def take(recv):
        pack[...] = recv[...].astype(F32).reshape(DEVICES * 8, CELLS)

    def shards(values):
        return values.astype(BF16).reshape(8, PER, CELLS)

    def whole(values):
        return values.reshape(CH, CELLS).astype(F32)

    def open_wide(wide, values, count):
        wide[: count * PER] = values.astype(F32).reshape(count * PER, CELLS)

    def channel(wide, k, count):
        values = wide[pl.ds(k, count, stride=PER), :]
        return jnp.concatenate([values[:, :RES], values[:, RES:]], axis=0).astype(BF16)

    def put_channel(wide, values, k, count):
        wide[pl.ds(k, count, stride=PER), :] = jnp.concatenate([values[:count], values[count:]], axis=1)

    def close_wide(wide, count):
        return wide[: count * PER].reshape(count, PER, CELLS).astype(BF16)

    def sum_groups(recv):
        total = jnp.sum(recv[...].astype(F32).reshape(4, CH, CELLS), axis=0)
        return total

    near_received(rights, 0)
    spread[...] = mul(
        right_all[...].reshape(RES * OUT, SEQ), left_own[...].reshape(ROWS * OUT, SEQ), NT
    ) * (1.0 / SEQ)
    for b in range(OUT):
        piece = spread[pl.ds(b, RES, stride=OUT), :].astype(BF16)
        for i in range(ROWS):
            outer_mean[i * RES : (i + 1) * RES, b * OUT : (b + 1) * OUT] = piece[:, i * OUT : (i + 1) * OUT]
    pair = pair + mul(outer_mean[...], mean_swapped_ref[...]).T

    def head(t, pair):
        normed, inverse = normalize(pair, 0)
        normed_s[t] = normed
        tail_s[t, 2, :1] = inverse
        projected = mul(triangle_t[t, : 4 * CH], normed.astype(BF16))
        parts_s[t, 0] = projected[:CH]
        parts_s[t, 1] = jax.nn.sigmoid(projected[CH : 2 * CH])
        parts_s[t, 2] = projected[2 * CH : 3 * CH]
        parts_s[t, 3] = jax.nn.sigmoid(projected[3 * CH : 4 * CH])
        return shards(parts_s[t, 0] * parts_s[t, 1]), shards(parts_s[t, 2] * parts_s[t, 3])

    def gate(t):
        gate_s[t] = jax.nn.sigmoid(mul(triangle_t[t, 4 * CH : 5 * CH], normed_s[t].astype(BF16)))

    def tail(t, pair, mixed):
        mixed_norm, mixed_inverse = normalize(mixed, 0)
        update = mul(triangle_t[t, 5 * CH :], mixed_norm.astype(BF16))
        tail_s[t, 0] = mixed_norm
        tail_s[t, 1] = update
        tail_s[t, 2, 8:9] = mixed_inverse
        return (pair + gate_s[t] * update).astype(BF16).astype(F32)

    pair = pair.astype(BF16).astype(F32)
    left_factor, right_factor = head(0, pair)
    right0_send[...] = right_factor
    exchange_global(right0_send, right0_recv, 2)
    left0_send[...] = left_factor
    exchange_near(left0_send, left0_recv, 3)
    gate(0)
    near_arrived(left0_recv, 3)
    open_wide(wide_a, left0_recv[...], 8)
    for k in range(PER):
        left0_chan[k] = channel(wide_a, k, 8)
    arrived(right0_recv, 2)
    open_wide(wide_b, right0_recv[...], DEVICES)
    for k in range(PER):
        right_k = channel(wide_b, k, DEVICES)
        right0_chan[k] = right_k
        put_channel(wide_c, mul(left0_chan[k], right_k, NT), k, 8)
    mixed0_send[...] = close_wide(wide_c, 8)
    exchange_near(mixed0_send, mixed0_recv, 4)
    gather_far(left_own, lefts, 27)
    near_arrived(mixed0_recv, 4)
    pair = tail(0, pair, whole(mixed0_recv[...]))

    left_factor, right_factor = head(1, pair)
    factor1_send[:, 0] = left_factor
    factor1_send[:, 1] = right_factor
    exchange_near(factor1_send, factor1_recv, 5)
    gate(1)
    near_arrived(factor1_recv, 5)
    open_wide(wide_a, factor1_recv[:, 0], 8)
    open_wide(wide_b, factor1_recv[:, 1], 8)
    for k in range(PER):
        left_k, right_k = channel(wide_a, k, 8), channel(wide_b, k, 8)
        left1_chan[k] = left_k
        right1_chan[k] = right_k
        put_channel(wide_c, mul(left_k, right_k, TN), k, DEVICES)
    mixed1_send[...] = close_wide(wide_c, DEVICES)
    exchange(mixed1_send, mixed1_recv, 6)
    forward_block(lefts, group, 1)
    arrived(mixed1_recv, 6)
    pair = tail(1, pair, sum_groups(mixed1_recv))
    updated_ref[...] = mul(order, pair.astype(BF16), NT).astype(BF16)

    def tail_back(t, upstream):
        gated = gate_s[t]
        mixed_norm = tail_s[t, 0]
        update_grad = (upstream * gated).astype(BF16)
        mixed_grad = norm_back(mixed_norm, tail_s[t, 2, 8:9], mul(mixing_ref[t], update_grad), 0)
        return update_grad, shards(mixed_grad)

    def tail_weights(t, upstream, update_grad):
        gated = gate_s[t]
        logit_grad = (upstream * tail_s[t, 1] * gated * (1.0 - gated)).astype(BF16)
        logit_s[t] = logit_grad
        mixing_grad = mul(tail_s[t, 0].astype(BF16), update_grad, NT).astype(BF16)
        return [mul(normed_s[t].astype(BF16), logit_grad, NT).astype(BF16), mixing_grad]

    def head_back(t, upstream, left_grad, right_grad):
        linear, switch = parts_s[t, 0], parts_s[t, 1]
        one = (left_grad * switch).astype(BF16)
        two = (left_grad * linear * switch * (1.0 - switch)).astype(BF16)
        linear, switch = parts_s[t, 2], parts_s[t, 3]
        three = (right_grad * switch).astype(BF16)
        four = (right_grad * linear * switch * (1.0 - switch)).astype(BF16)
        quarter = jnp.concatenate([one, two, three, four], axis=0)
        normed_grad = mul(triangle_ref[t], quarter) + mul(gating_ref[t], logit_s[t])
        return quarter, upstream + norm_back(normed_s[t], tail_s[t, 2, :1], normed_grad, 0)

    def head_weights(t, quarter):
        project_grad = mul(normed_s[t].astype(BF16), quarter, NT).astype(BF16)
        return [project_grad[:, q * CH : (q + 1) * CH] for q in range(4)]

    upstream = upstream_s[0]
    update_grad, back1_send[...] = tail_back(1, upstream)
    exchange_global(back1_send, back1_recv, 7)
    forward_arrived(lefts, 1, 27, 1)
    forward_arrived(lefts, 2, 27, 1)
    forward_arrived(lefts, 0, 27, 1)
    early = tail_weights(1, upstream, update_grad)
    arrived(back1_recv, 7)
    open_wide(wide_a, back1_recv[...], DEVICES)
    for k in range(PER):
        grad = channel(wide_a, k, DEVICES)
        put_channel(wide_b, mul(right1_chan[k], grad, NT), k, 8)
        put_channel(wide_c, mul(left1_chan[k], grad), k, 8)
    grad1_send[:, 0] = close_wide(wide_b, 8)
    grad1_send[:, 1] = close_wide(wide_c, 8)
    exchange_near(grad1_send, grad1_recv, 8)
    near_arrived(grad1_recv, 8)
    quarter, upstream = head_back(1, upstream, whole(grad1_recv[:, 0]), whole(grad1_recv[:, 1]))

    update_grad, back0_send[...] = tail_back(0, upstream)
    exchange_near(back0_send, back0_recv, 9)
    early += head_weights(1, quarter)
    early += tail_weights(0, upstream, update_grad)
    early_send[...] = jnp.concatenate(early, axis=0).reshape(GRID + (EARLY, CH))
    scatter_near(early_send, early_near, 13)
    near_arrived(back0_recv, 9)
    open_wide(wide_a, back0_recv[...], 8)
    grads = []
    for k in range(PER):
        grads.append(channel(wide_a, k, 8))
        put_channel(wide_b, mul(grads[k], left0_chan[k], TN), k, DEVICES)
    right_grad0_send[...] = close_wide(wide_b, DEVICES)
    exchange(right_grad0_send, right_grad0_recv, 45)
    for k in range(PER):
        put_channel(wide_c, mul(grads[k], right0_chan[k]), k, 8)
    left_grad0_send[...] = close_wide(wide_c, 8)
    exchange_near(left_grad0_send, left_grad0_recv, 44)
    scatter_far(early_send, early_near, early_class, early_far, 13, 14)
    near_arrived(left_grad0_recv, 44)
    arrived(right_grad0_recv, 45)
    quarter, upstream = head_back(0, upstream, whole(left_grad0_recv[...]), sum_groups(right_grad0_recv))

    cells = upstream.T
    own_cot = cells.astype(BF16)
    late = head_weights(0, quarter) + [mul(outer_mean[...], own_cot, TN).astype(BF16)]
    late_send[...] = jnp.concatenate(late, axis=0).reshape(GRID + (LATE, CH))
    scatter_near(late_send, late_near, 16)
    for k in range(4):
        pack[pl.ds(k, DEVICES, stride=8), :] = cells[k * DEVICES : (k + 1) * DEVICES]
    post(cot_send)
    exchange(cot_send, cot_recv, 10)
    for k in range(4):
        pair_grad_ref[pl.ds((k // 2) * RES + k % 2, DEVICES, stride=2), :] = cells[k * DEVICES : (k + 1) * DEVICES]
    received(early_far.at[pl.ds(1, 3)], 14)
    early_own[...] = jnp.sum(early_far[...].astype(F32), axis=0).astype(BF16)

    def factor_grad(cot, weight, factors):
        wide = (mul(cot, weight, NT) * (1.0 / SEQ)).astype(BF16).astype(F32)
        for b in range(OUT):
            piece = wide[:, b * OUT : (b + 1) * OUT]
            spread[pl.ds(b, RES, stride=OUT), :] = jnp.concatenate([piece[:RES], piece[RES:]], axis=1)
        return mul(spread[...].astype(BF16), factors[...].reshape(RES * OUT, SEQ), TN).astype(BF16)

    left_grad = factor_grad(own_cot, mean_swapped_ref[...], right_all)
    scatter_far(late_send, late_near, late_class, late_far, 16, 17)
    arrived(cot_recv, 10)
    take(cot_recv)
    theirs = [pack[pl.ds(k, DEVICES, stride=8), :] for k in range(4)]
    cot = jnp.concatenate([theirs[0], theirs[2], theirs[1], theirs[3]], axis=0).astype(BF16)
    near_received(lefts, 1)
    right_grad = factor_grad(cot, mean_ref[...], left_all)

    grads = [
        jnp.concatenate([left_grad[j * OUT : (j + 1) * OUT], right_grad[j * OUT : (j + 1) * OUT]], axis=0)
        for j in range(ROWS)
    ]
    outer_grad = sum(mul(grads[j], aligned[j].astype(BF16)) for j in range(ROWS))
    outer_grad = jnp.concatenate([outer_grad[:, :CH], outer_grad[:, CH:]], axis=0)
    outer_send[...] = outer_grad.astype(BF16).reshape(8, 16, CH)
    exchange_near(outer_send, outer_near, 11)
    for j in range(ROWS):
        back = mul(grads[j], outer_ref[...], TN)
        alignment_grad_ref[j] = norm_back(aligned[j], aligned_inv[j], back, 1)

    received(late_far.at[pl.ds(1, 3)], 17)
    late_own[:EARLY] = early_own[...]
    late_own[EARLY:] = jnp.sum(late_far[...].astype(F32), axis=0).astype(BF16)
    late_all[group, place] = late_own[...]
    gather_far(late_own, lates, 41)
    near_arrived(outer_near, 11)
    total = jnp.sum(outer_near[...].astype(F32), axis=0).astype(BF16)
    outer_part[...] = total
    for g in far_group:
        remote(outer_part, outer_far.at[group], 12, 8 * g + place).start()
    outer_far[group] = total
    gather_forward(lates, 41, 18)
    received(outer_far.at[pl.ds(0, 3)], 12)
    total = jnp.sum(outer_far[...].astype(F32), axis=0).astype(BF16)
    outer_own[...] = total
    for peer in near_peer:
        remote(outer_own, outer_all.at[place], 46, peer).start()
    outer_all[place] = total


    gather_left(rights, 20, 0)
    gather_left(lefts, 27, 1)
    sent(right0_recv, 2)
    near_sent(left0_recv, 3)
    near_sent(mixed0_recv, 4)
    near_sent(factor1_recv, 5)
    sent(mixed1_recv, 6)
    sent(back1_recv, 7)
    near_sent(grad1_recv, 8)
    near_sent(back0_recv, 9)
    near_sent(left_grad0_recv, 44)
    sent(right_grad0_recv, 45)
    sent(cot_recv, 10)
    near_sent(outer_near, 11)
    left(outer_far.at[pl.ds(0, 3)], 12)
    near_sent(outer_all, 46)
    scatter_left(early_near, early_far, 13, 14)
    scatter_left(late_near, late_far, 16, 17)

    near_arrived(outer_all, 46)
    outer = outer_all[...].reshape(CH, CH).astype(F32)
    outer_grad_ref[:, :CH] = outer[: 2 * OUT]
    outer_grad_ref[:, CH:] = outer[2 * OUT :]
    near_received(lates, 18)
    early_ref[...] = late_all[:, :, :EARLY].reshape(DEVICES * EARLY, CH)
    late_ref[...] = late_all[:, :, EARLY:].reshape(DEVICES * LATE, CH)
    gather_left(lates, 41, 18)


def finish(
    updated_ref, alignment_ref, pair_ref, outer_ref, early_ref, late_ref,
    updated_out, alignment_out, pair_out, outer_out, mean_out, triangle_out, gating_out, mixing_out,
):
    updated_out[...] = updated_ref[...]
    pair_out[...] = pair_ref[...]
    outer_out[...] = outer_ref[...]
    for j in range(ROWS):
        alignment_out[:, j, :] = alignment_ref[j]

    def early(k):
        return early_ref[k * CH : (k + 1) * CH].astype(F32)

    gating_out[1], mixing_out[1], gating_out[0], mixing_out[0] = early(0), early(1), early(6), early(7)
    for q in range(4):
        triangle_out[1, :, q * CH : (q + 1) * CH] = early(2 + q)
        triangle_out[0, :, q * CH : (q + 1) * CH] = late_ref[q * CH : (q + 1) * CH].astype(F32)
    for b in range(OUT):
        mean_out[pl.ds(b, OUT, stride=OUT), :] = late_ref[4 * CH + b * OUT : 4 * CH + (b + 1) * OUT].astype(F32)


def on_device(
    alignment, pair_features, pair_cotangent, outer_weight, mean_weight, triangle_weight, gating_weight, mixing_weight
):
    swapped = mean_weight.reshape(OUT, OUT, CH).swapaxes(0, 1).reshape(OUT * OUT, CH)

    def sums(rows):
        shapes = (GRID, (7, 4), (4,), (4,), (), GRID)
        return [pltpu.VMEM(shape + (rows, CH), BF16) for shape in shapes]

    near = pltpu.VMEM((8, PER, CELLS), BF16)
    near_two = pltpu.VMEM((8, 2, PER, CELLS), BF16)
    all_ = pltpu.VMEM((DEVICES, PER, CELLS), BF16)
    results = pl.pallas_call(
        kernel,
        out_shape=[
            jax.ShapeDtypeStruct((CELLS, CH), BF16),
            jax.ShapeDtypeStruct((ROWS, SEQ, MSA), F32),
            jax.ShapeDtypeStruct((CELLS, CH), F32),
            jax.ShapeDtypeStruct((2 * OUT, MSA), F32),
            jax.ShapeDtypeStruct((DEVICES * EARLY, CH), BF16),
            jax.ShapeDtypeStruct((DEVICES * LATE, CH), BF16),
        ],
        in_specs=[pl.BlockSpec(memory_space=pltpu.VMEM)] * 9,
        out_specs=[pl.BlockSpec(memory_space=pltpu.VMEM)] * 6,
        scratch_shapes=[
            pltpu.VMEM((ROWS, OUT, SEQ), BF16),
            pltpu.VMEM((ROWS, OUT, SEQ), BF16),
            pltpu.VMEM((ROWS,) + GRID + (OUT, SEQ), BF16),
            pltpu.VMEM((ROWS,) + GRID + (OUT, SEQ), BF16),
            pltpu.VMEM((ROWS, SEQ, MSA), F32),
            pltpu.VMEM((ROWS, SEQ, 1), F32),
            pltpu.VMEM((RES * OUT, ROWS * OUT), F32),
            pltpu.VMEM((CELLS, OUT * OUT), BF16),
            pltpu.VMEM((DEVICES * 8, CELLS), F32),
            pltpu.VMEM((DEVICES * PER, CELLS), F32),
            pltpu.VMEM((DEVICES * PER, CELLS), F32),
            pltpu.VMEM((DEVICES * PER, CELLS), F32),
            near, near, near, all_, near, near,
            near_two, near_two, all_, all_,
            near, all_, near_two, near_two,
            near, near, near, near, all_, all_,
            pltpu.VMEM((DEVICES, 8, CELLS), BF16),
            pltpu.VMEM((DEVICES, 8, CELLS), BF16),
            pltpu.VMEM((8, 16, CH), BF16),
            pltpu.VMEM((8, 16, CH), BF16),
            pltpu.VMEM((16, CH), BF16),
            pltpu.VMEM((4, 16, CH), BF16),
            pltpu.VMEM((16, CH), BF16),
            pltpu.VMEM((8, 16, CH), BF16),
            pltpu.VMEM((PER, 16, RES), BF16),
            pltpu.VMEM((PER, RES, RES), BF16),
            pltpu.VMEM((PER, 16, RES), BF16),
            pltpu.VMEM((PER, 16, RES), BF16),
            pltpu.VMEM((2, 6 * CH, CH), BF16),
            pltpu.VMEM((2, CH, CELLS), F32),
            pltpu.VMEM((2, 4, CH, CELLS), F32),
            pltpu.VMEM((2, CH, CELLS), F32),
            pltpu.VMEM((2, 3, CH, CELLS), F32),
            pltpu.VMEM((2, CH, CELLS), BF16),
            pltpu.VMEM((2, CH, CELLS), F32),
            *sums(EARLY)[:5],
            *sums(LATE)[:4],
            pltpu.VMEM((EARLY + LATE, CH), BF16),
            pltpu.VMEM(GRID + (EARLY + LATE, CH), BF16),
            pltpu.SemaphoreType.DMA((48,)),
            pltpu.SemaphoreType.DMA((48,)),
        ],
        compiler_params=pltpu.CompilerParams(
            collective_id=0, has_side_effects=True, vmem_limit_bytes=40 * 1024 * 1024
        ),
        name="evoformer",
    )(
        alignment.swapaxes(0, 1),
        pair_features.reshape(CELLS, CH),
        pair_cotangent.reshape(CELLS, CH),
        outer_weight.T,
        mean_weight,
        swapped,
        triangle_weight,
        gating_weight,
        mixing_weight,
    )

    updated, alignment_grad, pair_grad, outer_grad, mean_grad, triangle_grad, gating_grad, mixing_grad = pl.pallas_call(
        finish,
        out_shape=[
            jax.ShapeDtypeStruct((CELLS, CH), BF16),
            jax.ShapeDtypeStruct((SEQ, ROWS, MSA), F32),
            jax.ShapeDtypeStruct((CELLS, CH), F32),
            jax.ShapeDtypeStruct((2 * OUT, MSA), F32),
            jax.ShapeDtypeStruct((OUT * OUT, CH), F32),
            jax.ShapeDtypeStruct((2, CH, 4 * CH), F32),
            jax.ShapeDtypeStruct((2, CH, CH), F32),
            jax.ShapeDtypeStruct((2, CH, CH), F32),
        ],
        in_specs=[pl.BlockSpec(memory_space=pltpu.VMEM)] * 6,
        out_specs=[pl.BlockSpec(memory_space=pltpu.VMEM)] * 8,
        compiler_params=pltpu.CompilerParams(vmem_limit_bytes=24 * 1024 * 1024),
        name="finish",
    )(*results)
    return (
        updated.reshape(ROWS, RES, CH),
        alignment_grad,
        pair_grad.reshape(ROWS, RES, CH),
        outer_grad.T,
        mean_grad,
        triangle_grad,
        gating_grad,
        mixing_grad,
    )


def solution(mesh):
    in_specs = (
        P("crop", "res", None),
        P("res", "crop", None),
        P("res", "crop", None),
        P(),
        P(),
        P(),
        P(),
        P(),
    )
    out_specs = (
        P("res", "crop", None),
        P("crop", "res", None),
        P("res", "crop", None),
        P("crop", None),
        P("crop", None),
        P("crop", None, None),
        P("crop", None, None),
        P("crop", None, None),
    )
    return jax.shard_map(
        on_device, mesh=mesh, in_specs=in_specs, out_specs=out_specs, check_vma=False
    )
```

```python
import functools

import jax
import jax.numpy as jnp
from jax import lax
from jax.experimental import pallas as pl
from jax.experimental.pallas import tpu as pltpu
from jax.sharding import PartitionSpec as P

EPS = 1e-05
F32 = jnp.float32
BF16 = jnp.bfloat16
MESH = pl.DeviceIdType.MESH

DEVICES = 32
ROWS = 2
RES = DEVICES * ROWS
CELLS = ROWS * RES
CH = 128
OUT = 32
SEQ = 128
MSA = 256
PER = CH // 8
EARLY = 32
LATE = 48
CHIPS = 16
FAR = (2, 1, 3)
NEAR = ((2, 1), (1, 1), (3, 1), (2, 0), (1, 0), (3, 0), (0, 1))
GRID = (4, 8)

NN = (((1,), (0,)), ((), ()))
NT = (((1,), (1,)), ((), ()))
TN = (((0,), (0,)), ((), ()))


def mul(a, b, dims=NN):
    return lax.dot_general(a, b, dims, preferred_element_type=F32)


def normalize(values, axis):
    shifted = values - jnp.mean(values, axis=axis, keepdims=True)
    inverse = lax.rsqrt(jnp.mean(shifted * shifted, axis=axis, keepdims=True) + EPS)
    return shifted * inverse, inverse


def norm_back(normed, inverse, upstream, axis):
    mean_upstream = jnp.mean(upstream, axis=axis, keepdims=True)
    mean_product = jnp.mean(upstream * normed, axis=axis, keepdims=True)
    return inverse * (upstream - mean_upstream - normed * mean_product)


def kernel(
    alignment_ref, pair_ref, cotangent_ref, outer_ref, mean_ref, mean_swapped_ref, triangle_ref, gating_ref, mixing_ref,
    updated_ref, alignment_grad_ref, pair_grad_ref, outer_grad_ref, early_ref, late_ref,
    left_own, right_own, left_all, right_all, aligned, aligned_inv, spread, outer_mean, pack,
    wide_a, wide_b, wide_c,
    left0_send, left0_recv, right0_send, right0_recv, mixed0_send, mixed0_recv,
    factor1_send, factor1_recv, mixed1_send, mixed1_recv,
    back1_send, back1_recv, grad1_send, grad1_recv,
    back0_send, back0_recv, left_grad0_send, left_grad0_recv, right_grad0_send, right_grad0_recv,
    cot_send, cot_recv,
    outer_send, outer_near, outer_part, outer_far, outer_own, outer_all,
    left0_chan, right0_chan, left1_chan, right1_chan, triangle_t, normed_s, parts_s, gate_s, tail_s, logit_s, upstream_s,
    early_send, early_near, early_class, early_far, early_own,
    late_send, late_near, late_class, late_far, late_own, late_all,
    send_sem, recv_sem,
):
    me = lax.axis_index("res")
    other = lax.rem(me + 1, DEVICES)
    z, x = me // 2, lax.rem(me, 2)
    group, kind, place = me // 8, lax.rem(z, 4), lax.rem(me, 8)

    def each_peer(body):
        body(lax.rem(me + DEVICES // 2, DEVICES))

        def step(k, carry):
            body(lax.rem(me + DEVICES // 2 + k, DEVICES))
            body(lax.rem(me + DEVICES // 2 - k, DEVICES))
            return carry

        lax.fori_loop(1, DEVICES // 2, step, 0)

    def remote(source, target, phase, peer):
        return pltpu.make_async_remote_copy(
            src_ref=source, dst_ref=target, send_sem=send_sem.at[phase], recv_sem=recv_sem.at[phase],
            device_id={"res": peer}, device_id_type=MESH,
        )

    def received(view, phase):
        remote(view, view, phase, other).wait_recv()

    def left(view, phase):
        remote(view, view, phase, other).wait_send()

    def exchange(send, recv, phase):
        each_peer(lambda peer: remote(send.at[peer], recv.at[me], phase, peer).start())
        recv[me] = send[me]

    def exchange_global(send, recv, phase):
        each_peer(lambda peer: remote(send.at[lax.rem(peer, 8)], recv.at[me], phase, peer).start())
        recv[me] = send[place]

    def exchange_near(send, recv, phase):
        for n, peer in enumerate(near_peer):
            remote(send.at[near_place[n]], recv.at[place], phase, peer).start()
        recv[place] = send[place]

    def near_arrived(recv, phase):
        received(recv.at[pl.ds(0, 7)], phase)

    def near_sent(recv, phase):
        left(recv.at[pl.ds(0, 7)], phase)

    def arrived(recv, phase):
        received(recv.at[pl.ds(0, DEVICES - 1)], phase)

    def sent(recv, phase):
        left(recv.at[pl.ds(0, DEVICES - 1)], phase)

    far_group = [lax.rem(group + m, 4) for m in FAR]
    far_source = [lax.rem(group + 4 - m, 4) for m in FAR]
    steps = {0: 0, 1: 1, 3: CHIPS - 1, 2: CHIPS + 2 - 4 * (kind // 2)}
    near_x = [1 - x if flip else x for _, flip in NEAR]
    near_place = [lax.rem(kind + step, 4) * 2 + xx for (step, _), xx in zip(NEAR, near_x)]
    near_peer = [lax.rem(z + steps[step], CHIPS) * 2 + xx for (step, _), xx in zip(NEAR, near_x)]

    def gather_far(own, whole, phase):
        for k, g in enumerate(far_group):
            remote(own, whole(group, place), phase + k, 8 * g + place).start()

    def gather_near(whole, phase):
        for peer in near_peer:
            remote(whole(slice(None), place), whole(slice(None), place), phase, peer).start()

    def forward_block(whole, g, phase):
        for peer in near_peer:
            remote(whole(g, place), whole(g, place), phase, peer).start()

    def forward_arrived(whole, k, far_phase, phase):
        received(whole(far_source[k], place), far_phase + k)
        forward_block(whole, far_source[k], phase)

    def gather_forward(whole, far_phase, phase):
        for k in reversed(range(len(FAR))):
            forward_arrived(whole, k, far_phase, phase)

    def far_received(whole, phase):
        for k, g in enumerate(far_source):
            received(whole(g, place), phase + k)

    def gather_left(whole, far_phase, phase):
        for k, g in enumerate(far_source):
            left(whole(g, place), far_phase + k)
        left(whole(slice(None), pl.ds(0, 7)), phase)

    def near_received(whole, phase):
        received(whole(slice(None), pl.ds(0, 7)), phase)

    def scatter_near(send, near, phase):
        for n, peer in enumerate(near_peer):
            remote(send.at[:, near_place[n]], near.at[n], phase, peer).start()

    def scatter_far(send, near, of_place, far, near_phase, phase):
        received(near, near_phase)
        of_place[...] = (send[:, place].astype(F32) + jnp.sum(near[...].astype(F32), axis=0)).astype(BF16)
        for k, g in enumerate(far_group):
            remote(of_place.at[g], far.at[k + 1], phase, 8 * g + place).start()
        far[0] = of_place[group]

    def scatter_sum(far, own, whole, phase):
        received(far.at[pl.ds(1, 3)], phase)
        total = jnp.sum(far[...].astype(F32), axis=0).astype(BF16)
        own[...] = total
        whole[group, place] = total

    def scatter_left(near, far, near_phase, phase):
        left(near, near_phase)
        left(far.at[pl.ds(1, 3)], phase)

    rights = lambda g, e: right_all.at[:, g, e]
    lefts = lambda g, e: left_all.at[:, g, e]
    lates = lambda g, e: late_all.at[g, e]

    barrier = pltpu.get_barrier_semaphore()
    each_peer(lambda peer: pl.semaphore_signal(barrier, inc=1, device_id={"res": peer}, device_id_type=MESH))

    for j in range(ROWS):
        normed, inverse = normalize(alignment_ref[j].astype(F32), 1)
        aligned[j] = normed
        aligned_inv[j] = inverse
        projected = mul(outer_ref[...], normed.astype(BF16), NT).astype(BF16)
        left_own[j] = projected[:OUT]
        right_own[j] = projected[OUT:]
    pl.semaphore_wait(barrier, DEVICES - 1)

    gather_far(right_own, rights, 20)
    right_all[:, group, place] = right_own[...]
    forward_block(rights, group, 0)
    left_all[:, group, place] = left_own[...]

    row = lax.broadcasted_iota(jnp.int32, (CELLS, CELLS), 0)
    column = lax.broadcasted_iota(jnp.int32, (CELLS, CELLS), 1)
    kept = (row // RES) * RES + lax.rem(row, 2) * DEVICES + lax.rem(row, RES) // 2
    order = jnp.where(kept == column, 1.0, 0.0).astype(BF16)
    pair = mul(pair_ref[...], order, TN)
    upstream_s[0] = mul(cotangent_ref[...], order, TN)
    for t in range(2):
        triangle_t[t, : 4 * CH] = triangle_ref[t].T
        triangle_t[t, 4 * CH : 5 * CH] = gating_ref[t].T
        triangle_t[t, 5 * CH :] = mixing_ref[t].T
    pack[...] = jnp.zeros_like(pack)
    gather_forward(rights, 20, 0)

    def post(send):
        send[...] = pack[...].reshape(DEVICES, 8, CELLS).astype(BF16)

    def take(recv):
        pack[...] = recv[...].astype(F32).reshape(DEVICES * 8, CELLS)

    def shards(values):
        return values.astype(BF16).reshape(8, PER, CELLS)

    def whole(values):
        return values.reshape(CH, CELLS).astype(F32)

    def open_wide(wide, values, count):
        wide[: count * PER] = values.astype(F32).reshape(count * PER, CELLS)

    def channel(wide, k, count):
        values = wide[pl.ds(k, count, stride=PER), :]
        return jnp.concatenate([values[:, :RES], values[:, RES:]], axis=0).astype(BF16)

    def put_channel(wide, values, k, count):
        wide[pl.ds(k, count, stride=PER), :] = jnp.concatenate([values[:count], values[count:]], axis=1)

    def close_wide(wide, count):
        return wide[: count * PER].reshape(count, PER, CELLS).astype(BF16)

    def sum_groups(recv):
        total = jnp.sum(recv[...].astype(F32).reshape(4, CH, CELLS), axis=0)
        return total

    near_received(rights, 0)
    spread[...] = mul(
        right_all[...].reshape(RES * OUT, SEQ), left_own[...].reshape(ROWS * OUT, SEQ), NT
    ) * (1.0 / SEQ)
    for b in range(OUT):
        piece = spread[pl.ds(b, RES, stride=OUT), :].astype(BF16)
        for i in range(ROWS):
            outer_mean[i * RES : (i + 1) * RES, b * OUT : (b + 1) * OUT] = piece[:, i * OUT : (i + 1) * OUT]
    pair = pair + mul(outer_mean[...], mean_swapped_ref[...]).T

    def head(t, pair):
        normed, inverse = normalize(pair, 0)
        normed_s[t] = normed
        tail_s[t, 2, :1] = inverse
        projected = mul(triangle_t[t, : 4 * CH], normed.astype(BF16))
        parts_s[t, 0] = projected[:CH]
        parts_s[t, 1] = jax.nn.sigmoid(projected[CH : 2 * CH])
        parts_s[t, 2] = projected[2 * CH : 3 * CH]
        parts_s[t, 3] = jax.nn.sigmoid(projected[3 * CH : 4 * CH])
        return shards(parts_s[t, 0] * parts_s[t, 1]), shards(parts_s[t, 2] * parts_s[t, 3])

    def gate(t):
        gate_s[t] = jax.nn.sigmoid(mul(triangle_t[t, 4 * CH : 5 * CH], normed_s[t].astype(BF16)))

    def tail(t, pair, mixed):
        mixed_norm, mixed_inverse = normalize(mixed, 0)
        update = mul(triangle_t[t, 5 * CH :], mixed_norm.astype(BF16))
        tail_s[t, 0] = mixed_norm
        tail_s[t, 1] = update
        tail_s[t, 2, 8:9] = mixed_inverse
        return (pair + gate_s[t] * update).astype(BF16).astype(F32)

    pair = pair.astype(BF16).astype(F32)
    left_factor, right_factor = head(0, pair)
    right0_send[...] = right_factor
    exchange_global(right0_send, right0_recv, 2)
    left0_send[...] = left_factor
    exchange_near(left0_send, left0_recv, 3)
    gate(0)
    near_arrived(left0_recv, 3)
    open_wide(wide_a, left0_recv[...], 8)
    for k in range(PER):
        left0_chan[k] = channel(wide_a, k, 8)
    arrived(right0_recv, 2)
    open_wide(wide_b, right0_recv[...], DEVICES)
    for k in range(PER):
        right_k = channel(wide_b, k, DEVICES)
        right0_chan[k] = right_k
        put_channel(wide_c, mul(left0_chan[k], right_k, NT), k, 8)
    mixed0_send[...] = close_wide(wide_c, 8)
    exchange_near(mixed0_send, mixed0_recv, 4)
    gather_far(left_own, lefts, 27)
    near_arrived(mixed0_recv, 4)
    pair = tail(0, pair, whole(mixed0_recv[...]))

    left_factor, right_factor = head(1, pair)
    factor1_send[:, 0] = left_factor
    factor1_send[:, 1] = right_factor
    exchange_near(factor1_send, factor1_recv, 5)
    gate(1)
    near_arrived(factor1_recv, 5)
    open_wide(wide_a, factor1_recv[:, 0], 8)
    open_wide(wide_b, factor1_recv[:, 1], 8)
    for k in range(PER):
        left_k, right_k = channel(wide_a, k, 8), channel(wide_b, k, 8)
        left1_chan[k] = left_k
        right1_chan[k] = right_k
        put_channel(wide_c, mul(left_k, right_k, TN), k, DEVICES)
    mixed1_send[...] = close_wide(wide_c, DEVICES)
    exchange(mixed1_send, mixed1_recv, 6)
    forward_block(lefts, group, 1)
    arrived(mixed1_recv, 6)
    pair = tail(1, pair, sum_groups(mixed1_recv))
    updated_ref[...] = mul(order, pair.astype(BF16), NT).astype(BF16)

    def tail_back(t, upstream):
        gated = gate_s[t]
        mixed_norm = tail_s[t, 0]
        update_grad = (upstream * gated).astype(BF16)
        mixed_grad = norm_back(mixed_norm, tail_s[t, 2, 8:9], mul(mixing_ref[t], update_grad), 0)
        return update_grad, shards(mixed_grad)

    def tail_weights(t, upstream, update_grad):
        gated = gate_s[t]
        logit_grad = (upstream * tail_s[t, 1] * gated * (1.0 - gated)).astype(BF16)
        logit_s[t] = logit_grad
        mixing_grad = mul(tail_s[t, 0].astype(BF16), update_grad, NT).astype(BF16)
        return [mul(normed_s[t].astype(BF16), logit_grad, NT).astype(BF16), mixing_grad]

    def head_back(t, upstream, left_grad, right_grad):
        linear, switch = parts_s[t, 0], parts_s[t, 1]
        one = (left_grad * switch).astype(BF16)
        two = (left_grad * linear * switch * (1.0 - switch)).astype(BF16)
        linear, switch = parts_s[t, 2], parts_s[t, 3]
        three = (right_grad * switch).astype(BF16)
        four = (right_grad * linear * switch * (1.0 - switch)).astype(BF16)
        quarter = jnp.concatenate([one, two, three, four], axis=0)
        normed_grad = mul(triangle_ref[t], quarter) + mul(gating_ref[t], logit_s[t])
        return quarter, upstream + norm_back(normed_s[t], tail_s[t, 2, :1], normed_grad, 0)

    def head_weights(t, quarter):
        project_grad = mul(normed_s[t].astype(BF16), quarter, NT).astype(BF16)
        return [project_grad[:, q * CH : (q + 1) * CH] for q in range(4)]

    upstream = upstream_s[0]
    update_grad, back1_send[...] = tail_back(1, upstream)
    exchange_global(back1_send, back1_recv, 7)
    forward_arrived(lefts, 1, 27, 1)
    forward_arrived(lefts, 2, 27, 1)
    forward_arrived(lefts, 0, 27, 1)
    early = tail_weights(1, upstream, update_grad)
    arrived(back1_recv, 7)
    open_wide(wide_a, back1_recv[...], DEVICES)
    for k in range(PER):
        grad = channel(wide_a, k, DEVICES)
        put_channel(wide_b, mul(right1_chan[k], grad, NT), k, 8)
        put_channel(wide_c, mul(left1_chan[k], grad), k, 8)
    grad1_send[:, 0] = close_wide(wide_b, 8)
    grad1_send[:, 1] = close_wide(wide_c, 8)
    exchange_near(grad1_send, grad1_recv, 8)
    near_arrived(grad1_recv, 8)
    quarter, upstream = head_back(1, upstream, whole(grad1_recv[:, 0]), whole(grad1_recv[:, 1]))

    update_grad, back0_send[...] = tail_back(0, upstream)
    exchange_near(back0_send, back0_recv, 9)
    early += head_weights(1, quarter)
    early += tail_weights(0, upstream, update_grad)
    early_send[...] = jnp.concatenate(early, axis=0).reshape(GRID + (EARLY, CH))
    scatter_near(early_send, early_near, 13)
    near_arrived(back0_recv, 9)
    open_wide(wide_a, back0_recv[...], 8)
    grads = []
    for k in range(PER):
        grads.append(channel(wide_a, k, 8))
        put_channel(wide_b, mul(grads[k], left0_chan[k], TN), k, DEVICES)
    right_grad0_send[...] = close_wide(wide_b, DEVICES)
    exchange(right_grad0_send, right_grad0_recv, 45)
    for k in range(PER):
        put_channel(wide_c, mul(grads[k], right0_chan[k]), k, 8)
    left_grad0_send[...] = close_wide(wide_c, 8)
    exchange_near(left_grad0_send, left_grad0_recv, 44)
    scatter_far(early_send, early_near, early_class, early_far, 13, 14)
    near_arrived(left_grad0_recv, 44)
    arrived(right_grad0_recv, 45)
    quarter, upstream = head_back(0, upstream, whole(left_grad0_recv[...]), sum_groups(right_grad0_recv))

    cells = upstream.T
    own_cot = cells.astype(BF16)
    late = head_weights(0, quarter) + [mul(outer_mean[...], own_cot, TN).astype(BF16)]
    late_send[...] = jnp.concatenate(late, axis=0).reshape(GRID + (LATE, CH))
    scatter_near(late_send, late_near, 16)
    for k in range(4):
        pack[pl.ds(k, DEVICES, stride=8), :] = cells[k * DEVICES : (k + 1) * DEVICES]
    post(cot_send)
    exchange(cot_send, cot_recv, 10)
    for k in range(4):
        pair_grad_ref[pl.ds((k // 2) * RES + k % 2, DEVICES, stride=2), :] = cells[k * DEVICES : (k + 1) * DEVICES]
    received(early_far.at[pl.ds(1, 3)], 14)
    early_own[...] = jnp.sum(early_far[...].astype(F32), axis=0).astype(BF16)

    def factor_grad(cot, weight, factors):
        wide = (mul(cot, weight, NT) * (1.0 / SEQ)).astype(BF16).astype(F32)
        for b in range(OUT):
            piece = wide[:, b * OUT : (b + 1) * OUT]
            spread[pl.ds(b, RES, stride=OUT), :] = jnp.concatenate([piece[:RES], piece[RES:]], axis=1)
        return mul(spread[...].astype(BF16), factors[...].reshape(RES * OUT, SEQ), TN).astype(BF16)

    left_grad = factor_grad(own_cot, mean_swapped_ref[...], right_all)
    scatter_far(late_send, late_near, late_class, late_far, 16, 17)
    arrived(cot_recv, 10)
    take(cot_recv)
    theirs = [pack[pl.ds(k, DEVICES, stride=8), :] for k in range(4)]
    cot = jnp.concatenate([theirs[0], theirs[2], theirs[1], theirs[3]], axis=0).astype(BF16)
    near_received(lefts, 1)
    right_grad = factor_grad(cot, mean_ref[...], left_all)

    grads = [
        jnp.concatenate([left_grad[j * OUT : (j + 1) * OUT], right_grad[j * OUT : (j + 1) * OUT]], axis=0)
        for j in range(ROWS)
    ]
    outer_grad = sum(mul(grads[j], aligned[j].astype(BF16)) for j in range(ROWS))
    outer_grad = jnp.concatenate([outer_grad[:, :CH], outer_grad[:, CH:]], axis=0)
    outer_send[...] = outer_grad.astype(BF16).reshape(8, 16, CH)
    exchange_near(outer_send, outer_near, 11)
    for j in range(ROWS):
        back = mul(grads[j], outer_ref[...], TN)
        alignment_grad_ref[j] = norm_back(aligned[j], aligned_inv[j], back, 1)

    received(late_far.at[pl.ds(1, 3)], 17)
    late_own[:EARLY] = early_own[...]
    late_own[EARLY:] = jnp.sum(late_far[...].astype(F32), axis=0).astype(BF16)
    late_all[group, place] = late_own[...]
    gather_far(late_own, lates, 41)
    forward_block(lates, group, 18)
    near_arrived(outer_near, 11)
    total = jnp.sum(outer_near[...].astype(F32), axis=0).astype(BF16)
    outer_part[...] = total
    for g in far_group:
        remote(outer_part, outer_far.at[group], 12, 8 * g + place).start()
    outer_far[group] = total
    gather_forward(lates, 41, 18)
    received(outer_far.at[pl.ds(0, 3)], 12)
    total = jnp.sum(outer_far[...].astype(F32), axis=0).astype(BF16)
    outer_own[...] = total
    for peer in near_peer:
        remote(outer_own, outer_all.at[place], 46, peer).start()
    outer_all[place] = total


    gather_left(rights, 20, 0)
    gather_left(lefts, 27, 1)
    sent(right0_recv, 2)
    near_sent(left0_recv, 3)
    near_sent(mixed0_recv, 4)
    near_sent(factor1_recv, 5)
    sent(mixed1_recv, 6)
    sent(back1_recv, 7)
    near_sent(grad1_recv, 8)
    near_sent(back0_recv, 9)
    near_sent(left_grad0_recv, 44)
    sent(right_grad0_recv, 45)
    sent(cot_recv, 10)
    near_sent(outer_near, 11)
    left(outer_far.at[pl.ds(0, 3)], 12)
    near_sent(outer_all, 46)
    scatter_left(early_near, early_far, 13, 14)
    scatter_left(late_near, late_far, 16, 17)

    near_arrived(outer_all, 46)
    outer = outer_all[...].reshape(CH, CH).astype(F32)
    outer_grad_ref[:, :CH] = outer[: 2 * OUT]
    outer_grad_ref[:, CH:] = outer[2 * OUT :]
    near_received(lates, 18)
    early_ref[...] = late_all[:, :, :EARLY].reshape(DEVICES * EARLY, CH)
    late_ref[...] = late_all[:, :, EARLY:].reshape(DEVICES * LATE, CH)
    gather_left(lates, 41, 18)


def finish(
    updated_ref, alignment_ref, pair_ref, outer_ref, early_ref, late_ref,
    updated_out, alignment_out, pair_out, outer_out, mean_out, triangle_out, gating_out, mixing_out,
):
    updated_out[...] = updated_ref[...]
    pair_out[...] = pair_ref[...]
    outer_out[...] = outer_ref[...]
    for j in range(ROWS):
        alignment_out[:, j, :] = alignment_ref[j]

    def early(k):
        return early_ref[k * CH : (k + 1) * CH].astype(F32)

    gating_out[1], mixing_out[1], gating_out[0], mixing_out[0] = early(0), early(1), early(6), early(7)
    for q in range(4):
        triangle_out[1, :, q * CH : (q + 1) * CH] = early(2 + q)
        triangle_out[0, :, q * CH : (q + 1) * CH] = late_ref[q * CH : (q + 1) * CH].astype(F32)
    for b in range(OUT):
        mean_out[pl.ds(b, OUT, stride=OUT), :] = late_ref[4 * CH + b * OUT : 4 * CH + (b + 1) * OUT].astype(F32)


def on_device(
    alignment, pair_features, pair_cotangent, outer_weight, mean_weight, triangle_weight, gating_weight, mixing_weight
):
    swapped = mean_weight.reshape(OUT, OUT, CH).swapaxes(0, 1).reshape(OUT * OUT, CH)

    def sums(rows):
        shapes = (GRID, (7, 4), (4,), (4,), (), GRID)
        return [pltpu.VMEM(shape + (rows, CH), BF16) for shape in shapes]

    near = pltpu.VMEM((8, PER, CELLS), BF16)
    near_two = pltpu.VMEM((8, 2, PER, CELLS), BF16)
    all_ = pltpu.VMEM((DEVICES, PER, CELLS), BF16)
    results = pl.pallas_call(
        kernel,
        out_shape=[
            jax.ShapeDtypeStruct((CELLS, CH), BF16),
            jax.ShapeDtypeStruct((ROWS, SEQ, MSA), F32),
            jax.ShapeDtypeStruct((CELLS, CH), F32),
            jax.ShapeDtypeStruct((2 * OUT, MSA), F32),
            jax.ShapeDtypeStruct((DEVICES * EARLY, CH), BF16),
            jax.ShapeDtypeStruct((DEVICES * LATE, CH), BF16),
        ],
        in_specs=[pl.BlockSpec(memory_space=pltpu.VMEM)] * 9,
        out_specs=[pl.BlockSpec(memory_space=pltpu.VMEM)] * 6,
        scratch_shapes=[
            pltpu.VMEM((ROWS, OUT, SEQ), BF16),
            pltpu.VMEM((ROWS, OUT, SEQ), BF16),
            pltpu.VMEM((ROWS,) + GRID + (OUT, SEQ), BF16),
            pltpu.VMEM((ROWS,) + GRID + (OUT, SEQ), BF16),
            pltpu.VMEM((ROWS, SEQ, MSA), F32),
            pltpu.VMEM((ROWS, SEQ, 1), F32),
            pltpu.VMEM((RES * OUT, ROWS * OUT), F32),
            pltpu.VMEM((CELLS, OUT * OUT), BF16),
            pltpu.VMEM((DEVICES * 8, CELLS), F32),
            pltpu.VMEM((DEVICES * PER, CELLS), F32),
            pltpu.VMEM((DEVICES * PER, CELLS), F32),
            pltpu.VMEM((DEVICES * PER, CELLS), F32),
            near, near, near, all_, near, near,
            near_two, near_two, all_, all_,
            near, all_, near_two, near_two,
            near, near, near, near, all_, all_,
            pltpu.VMEM((DEVICES, 8, CELLS), BF16),
            pltpu.VMEM((DEVICES, 8, CELLS), BF16),
            pltpu.VMEM((8, 16, CH), BF16),
            pltpu.VMEM((8, 16, CH), BF16),
            pltpu.VMEM((16, CH), BF16),
            pltpu.VMEM((4, 16, CH), BF16),
            pltpu.VMEM((16, CH), BF16),
            pltpu.VMEM((8, 16, CH), BF16),
            pltpu.VMEM((PER, 16, RES), BF16),
            pltpu.VMEM((PER, RES, RES), BF16),
            pltpu.VMEM((PER, 16, RES), BF16),
            pltpu.VMEM((PER, 16, RES), BF16),
            pltpu.VMEM((2, 6 * CH, CH), BF16),
            pltpu.VMEM((2, CH, CELLS), F32),
            pltpu.VMEM((2, 4, CH, CELLS), F32),
            pltpu.VMEM((2, CH, CELLS), F32),
            pltpu.VMEM((2, 3, CH, CELLS), F32),
            pltpu.VMEM((2, CH, CELLS), BF16),
            pltpu.VMEM((2, CH, CELLS), F32),
            *sums(EARLY)[:5],
            *sums(LATE)[:4],
            pltpu.VMEM((EARLY + LATE, CH), BF16),
            pltpu.VMEM(GRID + (EARLY + LATE, CH), BF16),
            pltpu.SemaphoreType.DMA((48,)),
            pltpu.SemaphoreType.DMA((48,)),
        ],
        compiler_params=pltpu.CompilerParams(
            collective_id=0, has_side_effects=True, vmem_limit_bytes=40 * 1024 * 1024
        ),
        name="evoformer",
    )(
        alignment.swapaxes(0, 1),
        pair_features.reshape(CELLS, CH),
        pair_cotangent.reshape(CELLS, CH),
        outer_weight.T,
        mean_weight,
        swapped,
        triangle_weight,
        gating_weight,
        mixing_weight,
    )

    updated, alignment_grad, pair_grad, outer_grad, mean_grad, triangle_grad, gating_grad, mixing_grad = pl.pallas_call(
        finish,
        out_shape=[
            jax.ShapeDtypeStruct((CELLS, CH), BF16),
            jax.ShapeDtypeStruct((SEQ, ROWS, MSA), F32),
            jax.ShapeDtypeStruct((CELLS, CH), F32),
            jax.ShapeDtypeStruct((2 * OUT, MSA), F32),
            jax.ShapeDtypeStruct((OUT * OUT, CH), F32),
            jax.ShapeDtypeStruct((2, CH, 4 * CH), F32),
            jax.ShapeDtypeStruct((2, CH, CH), F32),
            jax.ShapeDtypeStruct((2, CH, CH), F32),
        ],
        in_specs=[pl.BlockSpec(memory_space=pltpu.VMEM)] * 6,
        out_specs=[pl.BlockSpec(memory_space=pltpu.VMEM)] * 8,
        compiler_params=pltpu.CompilerParams(vmem_limit_bytes=24 * 1024 * 1024),
        name="finish",
    )(*results)
    return (
        updated.reshape(ROWS, RES, CH),
        alignment_grad,
        pair_grad.reshape(ROWS, RES, CH),
        outer_grad.T,
        mean_grad,
        triangle_grad,
        gating_grad,
        mixing_grad,
    )


def solution(mesh):
    in_specs = (
        P("crop", "res", None),
        P("res", "crop", None),
        P("res", "crop", None),
        P(),
        P(),
        P(),
        P(),
        P(),
    )
    out_specs = (
        P("res", "crop", None),
        P("crop", "res", None),
        P("res", "crop", None),
        P("crop", None),
        P("crop", None),
        P("crop", None, None),
        P("crop", None, None),
        P("crop", None, None),
    )
    return jax.shard_map(
        on_device, mesh=mesh, in_specs=in_specs, out_specs=out_specs, check_vma=False
    )
```
